32 devices in a mesh: gz: 8 (over y, x, core), xy: 4 (over z).
Axes of the slice: x: 2, y: 2, z: 4, core: 2. Of those that a mesh axis runs over, the one named last changes fastest.
Arguments:
- flux_xface: bfloat16 [8, 2048, 2048], P(None, 'gz', 'xy'), may hold values from -6 to 6
- flux_yspec: bfloat16 [8, 2048, 2048], P(None, 'gz', 'xy'), may hold values from -6 to 6
- flux_zface: bfloat16 [8, 2048, 2048], P(None, 'gz', 'xy'), may hold values from -6 to 6
- frequency_y: int32 [8], replicated, may hold values from 0 to 2047
Outputs:
- potential: float32 [8, 2048, 2, 1024], P('gz', 'xy')
The draws below stay inside these ranges and needn't reach their ends.
All inputs are finite; a program needn't handle non-finite values.
Results may differ from the reference program's by a relative error of at most 0.0003.
Values may be sent and summed in bfloat16 or wider, within the bound.
No kernel may reach another device: no remote copies, remote signals or barrier semaphores. Data moves between devices by JAX's collectives and lax.ppermute only.
A program may use at most 64 MiB of HBM per device.

```python
import math
import jax
import jax.numpy as jnp
from jax import lax

NX = 2048
NY = 2048
NZ = 2048
YW = 8


def touch_ends(result, key, least, high):
    extent = result.shape
    spot = [jax.random.randint(jax.random.fold_in(key, axis), (), 0, extent[axis]) for axis in range(len(extent))]
    result = result.at[tuple(spot)].set(least)
    longest = extent.index(max(extent))
    spot[longest] = (spot[longest] + 1) % extent[longest]
    return result.at[tuple(spot)].set(high)


def levels(stream_key, shape, cuts, low, high):
    def one(axis_at, blocks):
        draws = jax.random.uniform(jax.random.fold_in(jax.random.fold_in(stream_key, 6), axis_at), (blocks,), jnp.float32, low / len(cuts), high / len(cuts))
        return jnp.repeat(jnp.exp(draws), shape[axis_at] // blocks).reshape((-1,) + (1,) * (len(shape) - axis_at - 1))

    factor_of = one(*cuts[0])
    for cut in cuts[1:]:
        factor_of = factor_of * one(*cut)
    return factor_of


def gaussian(own_key, extent, deviation, most, pieces=(), held_as=jnp.bfloat16):
    values = jax.random.normal(own_key, extent, jnp.float32) * deviation
    if len(pieces) > 0:
        values = levels(own_key, extent, pieces, -0.22, 0.18) * values
    return jnp.clip(values, min=-most, max=most).astype(held_as)


def setup_inputs(seed: int = 0) -> dict:
    key_list = jax.random.split(jax.random.key(seed), 5)
    flux_xface = gaussian(key_list[0], (YW, NZ, NX), 1.0, 6.0, ((1, 8), (2, 4)))
    flux_yspec = gaussian(key_list[1], (YW, NZ, NX), 1.0, 6.0, ((1, 8), (2, 4)))
    flux_zface = gaussian(key_list[2], (YW, NZ, NX), 1.0, 6.0, ((1, 8), (2, 4)))
    frequency_y = touch_ends(jax.random.randint(key_list[3], (YW,), 0, NY), jax.random.fold_in(key_list[3], 1), 0, NY - 1).astype(jnp.int32)
    return {"flux_xface": flux_xface, "flux_yspec": flux_yspec, "flux_zface": flux_zface, "frequency_y": frequency_y}


SCREEN_WEIGHT = 0.5

def cosine_transform(source, axis):
    moved = jnp.moveaxis(source, axis, -1)
    length = moved.shape[-1]
    reordered = jnp.concatenate([moved[..., 0::2], moved[..., 1::2][..., ::-1]], axis=-1)
    spectral = jnp.fft.fft(reordered, axis=-1)
    index_k = jnp.arange(length, dtype=jnp.int32)
    angle_k = math.pi / (2 * length) * index_k.astype(moved.dtype)
    real_part = jnp.cos(angle_k) * spectral.real + jnp.sin(angle_k) * spectral.imag
    scaling = jnp.where(index_k == 0, math.sqrt(1.0 / length), math.sqrt(2.0 / length)).astype(moved.dtype)
    return jnp.moveaxis(real_part * scaling, -1, axis)

def eigenvalue(length, dtype):
    sine = jnp.sin(jnp.arange(length, dtype=jnp.int32).astype(dtype) * (math.pi / (2 * length)))
    return 4.0 * sine * sine

def one_row(inputs):
    flux_x, flux_y, flux_z, frequency = inputs
    keep_x = (jnp.arange(NX, dtype=jnp.int32) < NX - 1).astype(jnp.float32)
    keep_z = (jnp.arange(NZ, dtype=jnp.int32) < NZ - 1).astype(jnp.float32)
    masked_x = flux_x.astype(jnp.float32) * keep_x[None, :]
    masked_z = flux_z.astype(jnp.float32) * keep_z[:, None]
    diff_x = masked_x - jnp.concatenate([jnp.zeros((NZ, 1), jnp.float32), masked_x[:, :-1]], axis=1)
    diff_z = masked_z - jnp.concatenate([jnp.zeros((1, NX), jnp.float32), masked_z[:-1]], axis=0)
    weight = 2.0 * jnp.sin(frequency.astype(jnp.float32) * (math.pi / (2 * NY)))
    divergence = diff_x + diff_z + weight * flux_y.astype(jnp.float32)
    spectrum = cosine_transform(cosine_transform(divergence, 0), 1)
    lam_z = eigenvalue(NZ, jnp.float32)
    lam_x = eigenvalue(NX, jnp.float32)
    denominator = weight * weight + lam_z[:, None] + lam_x[None, :] + SCREEN_WEIGHT
    potential = -spectrum / denominator
    return jnp.transpose(potential.reshape(NZ, NX // 2, 2), (0, 2, 1))

def reference(flux_xface, flux_yspec, flux_zface, frequency_y):
    return lax.map(one_row, (flux_xface, flux_yspec, flux_zface, frequency_y))
```

```python
import functools
import math

import jax
import jax.numpy as jnp
import numpy as np
from jax import lax
from jax.experimental import pallas as pl
from jax.experimental.pallas import tpu as pltpu
from jax.sharding import PartitionSpec as P

NX = 2048
NY = 2048
NZ = 2048


SCREEN_WEIGHT = 0.5


def shifted(block, axis, distance):
    devices = range(lax.axis_size(axis))
    route = [(i - distance, i) for i in devices if i - distance in devices]
    return lax.ppermute(block, axis, route)


def cosine_table(length, parity):
    halved = length // 2
    row_index = lax.broadcasted_iota(jnp.int32, (halved, halved), 0)
    col_index = lax.broadcasted_iota(jnp.int32, (halved, halved), 1)
    frequency = 2 * row_index + parity
    phase = frequency * (2 * col_index + 1) % (4 * length)
    scaling = jnp.where(frequency == 0, math.sqrt(1.0 / length), math.sqrt(2.0 / length)).astype(
        jnp.float32
    )
    return scaling * jnp.cos(phase.astype(jnp.float32) * (math.pi / (2 * length)))


def fold_middle(source):
    length = source.shape[1]
    halved = length // 2
    upper_half = source[:, :halved]
    lower_half = lax.rev(source[:, halved:], (1,))
    even_part = jnp.einsum(
        "kq,fql->fkl",
        cosine_table(length, 0),
        upper_half + lower_half,
        precision=lax.Precision.HIGHEST,
    )
    odd_part = jnp.einsum(
        "kq,fql->fkl",
        cosine_table(length, 1),
        upper_half - lower_half,
        precision=lax.Precision.HIGHEST,
    )
    return jnp.stack([even_part, odd_part], axis=2).reshape(source.shape)


def fold_last(source):
    length = source.shape[2]
    halved = length // 2
    upper_half = source[:, :, :halved]
    lower_half = lax.rev(source[:, :, halved:], (2,))
    even_part = jnp.einsum(
        "yzn,mn->yzm",
        upper_half + lower_half,
        cosine_table(length, 0),
        precision=lax.Precision.HIGHEST,
    )
    odd_part = jnp.einsum(
        "yzn,mn->yzm",
        upper_half - lower_half,
        cosine_table(length, 1),
        precision=lax.Precision.HIGHEST,
    )
    return jnp.stack([even_part, odd_part], axis=2)


def eigenvalue(index, length):
    sine = jnp.sin(index.astype(jnp.float32) * (math.pi / (2 * length)))
    return 4.0 * sine * sine


def plain_shards(flux_xface, flux_yspec, flux_zface, frequency_y):
    x_rank = lax.axis_index("xy")
    x_count = lax.axis_size("xy")
    z_rank = lax.axis_index("gz")
    z_count = lax.axis_size("gz")
    planes = flux_xface.shape[1]
    x_width = flux_xface.shape[2]
    x_position = lax.broadcasted_iota(jnp.int32, flux_xface.shape, 2)
    x_keep = jnp.logical_not((x_rank == x_count - 1) & (x_position == x_width - 1))
    masked_x = jnp.where(x_keep, flux_xface, jnp.zeros_like(flux_xface))
    x_edge = shifted(masked_x[:, :, x_width - 1 :], "xy", 1)
    x_before = jnp.concatenate([x_edge, masked_x[:, :, : x_width - 1]], axis=2)
    weight_y = 2.0 * jnp.sin(frequency_y.astype(jnp.float32) * (math.pi / (2 * NY)))
    partial_value = (
        masked_x.astype(jnp.float32)
        - x_before.astype(jnp.float32)
        + weight_y[:, None, None] * flux_yspec.astype(jnp.float32)
    )
    z_position = lax.broadcasted_iota(jnp.int32, flux_zface.shape, 1)
    z_keep = jnp.logical_not((z_rank == z_count - 1) & (z_position == planes - 1))
    masked_z = jnp.where(z_keep, flux_zface, jnp.zeros_like(flux_zface))
    z_edge = shifted(masked_z[:, planes - 1 :, :], "gz", 1)
    z_before = jnp.concatenate([z_edge, masked_z[:, : planes - 1]], axis=1)
    slab = partial_value + masked_z.astype(jnp.float32) - z_before.astype(jnp.float32)
    totals = lax.all_to_all(slab, "gz", split_axis=0, concat_axis=1, tiled=True)
    spectrum_z = fold_middle(totals)
    x_lines = lax.all_to_all(spectrum_z, "xy", split_axis=1, concat_axis=2, tiled=True)
    spectrum = fold_last(x_lines)
    row_count = spectrum.shape[0]
    kz_count = spectrum.shape[1]
    halved = spectrum.shape[3]
    local_freq = lax.dynamic_slice_in_dim(frequency_y, z_rank * row_count, row_count)
    weight_local = 2.0 * jnp.sin(local_freq.astype(jnp.float32) * (math.pi / (2 * NY)))
    kz_index = x_rank * kz_count + lax.broadcasted_iota(jnp.int32, (kz_count,), 0)
    kx_index = 2 * lax.broadcasted_iota(jnp.int32, (2, halved), 1) + lax.broadcasted_iota(
        jnp.int32, (2, halved), 0
    )
    denominator = (
        (weight_local * weight_local)[:, None, None, None]
        + eigenvalue(kz_index, NZ)[None, :, None, None]
        + eigenvalue(kx_index, NX)[None, None, :, :]
        + SCREEN_WEIGHT
    )
    return -spectrum / denominator


LANES = 128
GROUP = 32
META = 16
STEPS = 64.0
TOP = 32700.0
BLOCKS = 8
RESIDUES = 2 * BLOCKS


def split_bf16(table):
    high = table.astype(jnp.bfloat16)
    low = (table - high.astype(np.float64)).astype(jnp.bfloat16)
    return np.stack([high, low])


def scaled_cosine(frequency, position, length, wave=np.cos):
    phase = (frequency[:, None] * (2 * position[None, :] + 1)) % (4 * length)
    scaling = np.where(frequency == 0, math.sqrt(1.0 / length), math.sqrt(2.0 / length))
    return scaling[:, None] * wave(phase * (math.pi / (2 * length)))


def z_tables(length):
    inner = np.arange(length // BLOCKS)
    outer = RESIDUES * np.arange(length // RESIDUES)
    pairs = []
    for r in range(1, BLOCKS):
        upper = [scaled_cosine(outer + r, inner, length), -scaled_cosine(outer + r, inner, length, np.sin)]
        mirror = outer + RESIDUES - r
        lower = [scaled_cosine(mirror, inner, length), scaled_cosine(mirror, inner, length, np.sin)]
        pairs.append(np.concatenate([np.concatenate(upper, axis=1), np.concatenate(lower, axis=1)], axis=0))
    ends = [scaled_cosine(outer, inner, length), scaled_cosine(outer + BLOCKS, inner, length)]
    return split_bf16(np.stack(pairs)), split_bf16(np.stack(ends))


def x_tables(length, positions):
    halved = length // 2
    tables = [scaled_cosine(2 * np.arange(halved) + p, positions, length).T for p in (0, 1)]
    return split_bf16(np.stack(tables))


def steps_of(largest):
    return jnp.ceil(jnp.log2(jnp.maximum(largest, 2.0**-100)) * STEPS)


def encoded(values, extra=None):
    largest = jnp.max(jnp.abs(values), axis=1)
    if extra is not None:
        largest = jnp.maximum(largest, extra)
    steps = steps_of(largest)
    factor = TOP * jnp.exp2(steps * (-1.0 / STEPS))
    return jnp.round(values * factor[:, None, :]).astype(jnp.int32), steps, factor


def decoded(codes, steps):
    scale = jnp.exp2(steps * (1.0 / STEPS)) * (1.0 / TOP)
    groups = steps.shape[0]
    values = codes.astype(jnp.int32).astype(jnp.float32).reshape(groups, GROUP, codes.shape[-1])
    return values * scale[:, None, :], scale


def divergence_kernel(tiles, has_edge, *refs):
    place, weight = refs[0], refs[1]
    flux_x, flux_y, flux_z = refs[2:5]
    rest = refs[5:]
    if has_edge:
        edge_in, *rest = rest
    outs = rest[:BLOCKS]
    z_rank, z_count, x_rank, x_count = place[0], place[1], place[2], place[3]
    step = pl.program_id(0)
    y = z_rank ^ step
    rows, width = flux_x.shape[1], flux_x.shape[2]
    last_tile = width // LANES - 1
    reverse = x_rank >= x_count // 2
    row_at = lax.broadcasted_iota(jnp.int32, (LANES, LANES), 0)
    col_at = lax.broadcasted_iota(jnp.int32, (LANES, LANES), 1)
    col_at = jnp.where(reverse, LANES - 1 - col_at, col_at)
    take = (row_at == col_at).astype(jnp.float32)
    below = (row_at + 1 == col_at).astype(jnp.float32)
    wrap = ((row_at == LANES - 1) & (col_at == 0)).astype(jnp.bfloat16)
    pick = take.astype(jnp.bfloat16)
    y_weight = weight[y]
    dot = functools.partial(jnp.dot, preferred_element_type=jnp.float32)
    z_last = jnp.where(z_rank == z_count - 1, rows - 1, rows)
    row_id = lax.broadcasted_iota(jnp.int32, (rows, LANES), 0)
    for at, tile in enumerate(tiles):
        source = jnp.where(reverse, last_tile - tile, tile)
        lanes = pl.ds(pl.multiple_of(source * LANES, LANES), LANES)
        drop_last = (x_rank == x_count - 1) & (source == last_tile)
        keep = jnp.where(drop_last & (row_at == LANES - 1), 0.0, take)
        value = dot(flux_x[0, :, lanes], (keep - below).astype(jnp.bfloat16))
        before = jnp.maximum(source - 1, 0)
        before_lanes = pl.ds(pl.multiple_of(before * LANES, LANES), LANES)
        wrap_here = wrap if not has_edge else jnp.where(source == 0, jnp.zeros_like(wrap), wrap)
        value -= dot(flux_x[0, :, before_lanes], wrap_here)
        if has_edge:
            halo_row = lax.broadcasted_iota(jnp.int32, (edge_in.shape[0], LANES), 0)
            halo_col = lax.broadcasted_iota(jnp.int32, (edge_in.shape[0], LANES), 1)
            halo_col = jnp.where(reverse, LANES - 1 - halo_col, halo_col)
            chosen = (halo_row == y) & (halo_col == 0) & (source == 0) & (x_rank > 0)
            value -= lax.dot_general(
                edge_in[...].astype(jnp.bfloat16),
                chosen.astype(jnp.bfloat16),
                (((0,), (0,)), ((), ())),
                preferred_element_type=jnp.float32,
            )
        value += y_weight * dot(flux_y[0, :, lanes], pick)
        face = jnp.where(row_id == z_last, 0.0, dot(flux_z[0, :, lanes], pick))
        face_before = jnp.where(row_id == 0, 0.0, pltpu.roll(face, 1, 0))
        value += face - face_before
        halo = -face[rows - 1 :]
        groups = rows // GROUP
        at_end = lax.broadcasted_iota(jnp.int32, (groups, LANES), 0) == groups - 1
        extra = jnp.where(at_end, jnp.abs(halo), 0.0)
        codes, steps, factor = encoded(value.reshape(groups, GROUP, LANES), extra)
        halo_code = jnp.round(halo * factor[groups - 1 :])
        filler = jnp.zeros((META - groups - 1, LANES), jnp.float32)
        meta = jnp.concatenate([steps, halo_code, filler], axis=0).astype(jnp.int32)
        message = jnp.concatenate([codes.reshape(rows, LANES), meta], axis=0).astype(jnp.int16)
        for d in range(BLOCKS):

            @pl.when(step == d)
            def _(d=d):
                outs[d][:, at * LANES : (at + 1) * LANES] = message

    if not has_edge:
        edge_out = rest[BLOCKS]
        ending = lax.broadcasted_iota(jnp.int32, (8, LANES), 1) == LANES - 1
        column = lax.dot_general(
            ending.astype(jnp.bfloat16),
            flux_x[0, :, width - LANES :],
            (((1,), (1,)), ((), ())),
            preferred_element_type=jnp.float32,
        )
        edge_out[pl.ds(y, 1), :] = column[:1]


def divergence(tiles, place, weight, fluxes, edge=None):
    y_count, rows, width = fluxes[0].shape
    chunk = len(tiles) * LANES
    out_shape = [jax.ShapeDtypeStruct((rows + META, chunk), jnp.int16)] * BLOCKS
    out_specs = [pl.BlockSpec((rows + META, chunk), lambda d, *_: (0, 0))] * BLOCKS
    in_specs = [pl.BlockSpec((1, rows, width), lambda d, place, weight: (place[0] ^ d, 0, 0))] * 3
    operands = list(fluxes)
    if edge is None:
        out_shape.append(jax.ShapeDtypeStruct((y_count, rows), jnp.float32))
        out_specs.append(pl.BlockSpec((y_count, rows), lambda d, *_: (0, 0)))
    else:
        in_specs.append(pl.BlockSpec((y_count, rows), lambda d, *_: (0, 0)))
        operands.append(edge)
    return pl.pallas_call(
        functools.partial(divergence_kernel, tiles, edge is not None),
        grid_spec=pltpu.PrefetchScalarGridSpec(
            num_scalar_prefetch=2, grid=(BLOCKS,), in_specs=in_specs, out_specs=out_specs
        ),
        out_shape=out_shape,
        compiler_params=pltpu.CompilerParams(vmem_limit_bytes=40 << 20),
        cost_estimate=pl.CostEstimate(
            flops=8 * y_count * rows * chunk * LANES, bytes_accessed=8 * y_count * rows * chunk, transcendentals=0
        ),
        name="divergence",
    )(place, weight, *operands)


def z_kernel(place, *refs):
    pieces = refs[:BLOCKS]
    pair_table, end_table = refs[BLOCKS : BLOCKS + 2]
    outs = refs[BLOCKS + 2 : -5]
    blocks, halos, high, low, result = refs[-5:]
    z_rank, x_rank = place[0], place[2]
    rows = blocks.shape[1]
    chunk = blocks.shape[2]
    groups = rows // GROUP
    for d in range(BLOCKS):
        source = z_rank ^ d
        meta = pieces[d][rows:, :].astype(jnp.int32).astype(jnp.float32)
        values, scale = decoded(pieces[d][:rows, :], meta[:groups])
        blocks[source] = values.reshape(rows, chunk)
        halos[pl.ds(source, 1), :] = meta[groups : groups + 1] * scale[groups - 1 :]
    for b in range(1, BLOCKS):
        blocks[b, :1, :] += halos[b - 1 : b, :]

    near, far, mid = math.cos(math.pi / 8), math.sin(math.pi / 8), math.sqrt(0.5)
    strip = 16

    def keep(r, part, start, value):
        spot = pl.ds(part * rows + start, strip)
        rounded = value.astype(jnp.bfloat16)
        high[r, spot, :] = rounded
        low[r, spot, :] = (value - rounded.astype(jnp.float32)).astype(jnp.bfloat16)

    def combine(i, carry):
        start = pl.multiple_of(i * strip, strip)
        v = [blocks[b, pl.ds(start, strip), :] for b in range(BLOCKS)]
        p1, p2, p3 = v[1] + v[7], v[2] + v[6], v[3] + v[5]
        n1, n2, n3 = v[1] - v[7], v[2] - v[6], v[3] - v[5]
        ends, gap = v[0] + v[4], v[0] - v[4]
        odd = p1 + p3
        even = ends + p2
        keep(0, 0, start, even + odd)
        keep(8, 0, start, even - odd)
        keep(4, 0, start, ends - p2)
        turn = mid * (p1 - p3)
        keep(2, 0, start, gap + turn)
        keep(6, 0, start, gap - turn)
        turn = mid * (n1 + n3)
        keep(2, 1, start, turn + n2)
        keep(6, 1, start, turn - n2)
        keep(4, 1, start, n1 - n3)
        m2 = mid * n2
        s, t = v[0] + m2, near * n1 + far * n3
        keep(1, 0, start, s + t)
        keep(7, 0, start, s - t)
        s, t = v[0] - m2, far * n1 - near * n3
        keep(3, 0, start, s + t)
        keep(5, 0, start, s - t)
        m2 = mid * p2
        s, t = far * p1 + near * p3, m2 + v[4]
        keep(1, 1, start, s + t)
        keep(7, 1, start, s - t)
        s, t = near * p1 - far * p3, m2 - v[4]
        keep(3, 1, start, s + t)
        keep(5, 1, start, s - t)
        return carry

    lax.fori_loop(0, rows // strip, combine, 0)
    dot = functools.partial(jnp.dot, preferred_element_type=jnp.float32)
    half = result.shape[1]
    for r in range(1, BLOCKS):
        value = dot(pair_table[0, r - 1], high[r])
        value += dot(pair_table[0, r - 1], low[r])
        value += dot(pair_table[1, r - 1], high[r])
        result[r] = value[:half]
        result[RESIDUES - r] = value[half:]
    for e, r in enumerate((0, BLOCKS)):
        value = dot(end_table[0, e], high[r, :rows, :])
        value += dot(end_table[0, e], low[r, :rows, :])
        value += dot(end_table[1, e], high[r, :rows, :])
        result[r] = value
    share = half // len(outs)
    per = share // GROUP
    for e, out in enumerate(outs):
        first = pl.multiple_of((x_rank ^ e) * share, GROUP)
        metas = []
        for r in range(RESIDUES):
            values = result[r, pl.ds(first, share), :].reshape(per, GROUP, chunk)
            codes, steps, _ = encoded(values)
            out[r * share : (r + 1) * share, :] = codes.reshape(share, chunk).astype(jnp.int16)
            metas.append(steps)
        out[RESIDUES * share :, :] = jnp.concatenate(metas, axis=0).astype(jnp.int32).astype(jnp.int16)


def z_transform(place, pieces, tables, x_count):
    rows = pieces[0].shape[0] - META
    chunk = pieces[0].shape[1]
    length = rows * BLOCKS
    out_rows = length // x_count + META
    vmem = pl.BlockSpec(memory_space=pltpu.VMEM)
    return pl.pallas_call(
        z_kernel,
        in_specs=[pl.BlockSpec(memory_space=pltpu.SMEM)] + [vmem] * (BLOCKS + 2),
        out_specs=[vmem] * x_count,
        out_shape=[jax.ShapeDtypeStruct((out_rows, chunk), jnp.int16)] * x_count,
        scratch_shapes=[
            pltpu.VMEM((BLOCKS, rows, chunk), jnp.float32),
            pltpu.VMEM((BLOCKS, chunk), jnp.float32),
            pltpu.VMEM((BLOCKS + 1, 2 * rows, chunk), jnp.bfloat16),
            pltpu.VMEM((BLOCKS + 1, 2 * rows, chunk), jnp.bfloat16),
            pltpu.VMEM((RESIDUES, length // RESIDUES, chunk), jnp.float32),
        ],
        compiler_params=pltpu.CompilerParams(vmem_limit_bytes=40 << 20),
        cost_estimate=pl.CostEstimate(
            flops=3 * length * length // 2 * chunk, bytes_accessed=8 * length * chunk, transcendentals=0
        ),
        name="z_transform",
    )(place, *pieces, *tables)


def x_kernel(last, *refs):
    place = refs[0]
    refs = refs[1:]
    x_count = 4
    pieces = refs[:x_count]
    table = refs[x_count]
    refs = refs[x_count + 1 :]
    if last:
        total, row_part, col_part, out, values, high, low = refs
    else:
        out, values, high, low = refs
    x_rank = place[2]
    rows, chunk = values.shape[2], values.shape[1] * LANES
    per = rows // RESIDUES // GROUP
    for e in range(x_count):
        source = x_rank ^ e
        steps = pieces[e][rows:, :].astype(jnp.int32).astype(jnp.float32)
        for r in range(RESIDUES):
            share = rows // RESIDUES
            part, _ = decoded(pieces[e][r * share : (r + 1) * share, :], steps[r * per : (r + 1) * per])
            part = part.reshape(share, chunk)
            for t in range(chunk // LANES):
                values[source, t, pl.ds(r, share, stride=RESIDUES), :] = part[:, t * LANES : (t + 1) * LANES]
    half = x_count // 2
    for j in range(half):
        for t in range(chunk // LANES):
            near, far = values[j, t], values[x_count - 1 - j, t]
            lanes = slice(j * chunk + t * LANES, j * chunk + (t + 1) * LANES)
            for p, value in enumerate((near + far, near - far)):
                rounded = value.astype(jnp.bfloat16)
                high[p, :, lanes] = rounded
                low[p, :, lanes] = (value - rounded.astype(jnp.float32)).astype(jnp.bfloat16)
    dot = functools.partial(jnp.dot, preferred_element_type=jnp.float32)
    count = table.shape[3]
    width = 256
    for p in range(2):
        for c in range(count // width):
            cols = slice(c * width, (c + 1) * width)
            value = dot(high[p], table[0, p, :, cols])
            value += dot(low[p], table[0, p, :, cols])
            value += dot(high[p], table[1, p, :, cols])
            if not last:
                out[p, :, cols] = value
                continue
            value += total[p, :, cols]
            for t in range(width // LANES):
                tile = c * (width // LANES) + t
                lanes = slice(tile * LANES, (tile + 1) * LANES)
                below = row_part[...] + col_part[p : p + 1, lanes]
                part = value[:, t * LANES : (t + 1) * LANES] / below
                per_row = 2 * count // LANES
                out[pl.ds(2 * tile + p, rows, stride=per_row), :] = part


def x_transform(place, pieces, table, ending=None):
    x_count = len(pieces)
    rows = pieces[0].shape[0] - META
    chunk = pieces[0].shape[1]
    count = table.shape[3]
    vmem = pl.BlockSpec(memory_space=pltpu.VMEM)
    last = ending is not None
    extra = list(ending) if last else []
    shape = (rows * 2 * count // LANES, LANES) if last else (2, rows, count)
    return pl.pallas_call(
        functools.partial(x_kernel, last),
        in_specs=[pl.BlockSpec(memory_space=pltpu.SMEM)] + [vmem] * (x_count + 1 + len(extra)),
        out_specs=vmem,
        out_shape=jax.ShapeDtypeStruct(shape, jnp.float32),
        scratch_shapes=[
            pltpu.VMEM((x_count, chunk // LANES, rows, LANES), jnp.float32),
            pltpu.VMEM((2, rows, x_count // 2 * chunk), jnp.bfloat16),
            pltpu.VMEM((2, rows, x_count // 2 * chunk), jnp.bfloat16),
        ],
        compiler_params=pltpu.CompilerParams(vmem_limit_bytes=40 << 20),
        cost_estimate=pl.CostEstimate(
            flops=6 * rows * x_count * chunk * count, bytes_accessed=16 * rows * count, transcendentals=0
        ),
        name="x_transform",
    )(place, *pieces, table, *extra)


def exchanged(pieces, axis, order):
    count = len(pieces)
    received = [pieces[0]] + [None] * (count - 1)
    for d in order:
        received[d] = lax.ppermute(pieces[d], axis, [(i, i ^ d) for i in range(count)])
    return received


def shards(flux_xface, flux_yspec, flux_zface, frequency_y):
    z_count = lax.axis_size("gz")
    x_count = lax.axis_size("xy")
    y_count, planes, x_width = flux_xface.shape
    length_z, length_x = planes * z_count, x_width * x_count
    fits = z_count == BLOCKS and y_count == BLOCKS and x_count == 4 and x_width == 4 * LANES
    if not fits or planes % GROUP or planes // GROUP >= META or length_z != RESIDUES * GROUP * x_count:
        return plain_shards(flux_xface, flux_yspec, flux_zface, frequency_y)
    z_rank, x_rank = lax.axis_index("gz"), lax.axis_index("xy")
    place = jnp.stack([z_rank, jnp.int32(z_count), x_rank, jnp.int32(x_count)]).astype(jnp.int32)
    weight_y = 2.0 * jnp.sin(frequency_y.astype(jnp.float32) * (math.pi / (2 * NY)))
    fluxes = (flux_xface, flux_yspec, flux_zface)
    inner, outer = (1, 2), (0, 3)
    tables_z = z_tables(length_z)
    order = (6, 7, 2, 4, 3, 5, 1)
    *first, edge = divergence(inner, place, weight_y, fluxes)
    edge_before = lax.ppermute(edge, "xy", [(i, i + 1) for i in range(x_count - 1)])
    lanes = np.arange(LANES)

    def positions(tiles):
        return np.concatenate([j * x_width + t * LANES + lanes for j in range(x_count // 2) for t in tiles])

    first = exchanged(first, "gz", order)
    second = divergence(outer, place, weight_y, fluxes, edge_before)
    second = exchanged(second, "gz", order)
    first = exchanged(z_transform(place, first, tables_z, x_count), "xy", (3, 2, 1))
    second = exchanged(z_transform(place, second, tables_z, x_count), "xy", (3, 2, 1))
    kz_count = length_z // x_count
    halved = length_x // 2
    local_weight = weight_y[z_rank]
    kz_index = x_rank * kz_count + lax.broadcasted_iota(jnp.int32, (kz_count, LANES), 0)
    row_part = -(local_weight * local_weight + eigenvalue(kz_index, length_z) + SCREEN_WEIGHT)
    kx_index = 2 * np.arange(halved)[None, :] + np.arange(2)[:, None]
    col_part = np.asarray(-4.0 * np.sin(kx_index * (math.pi / (2 * length_x))) ** 2, np.float32)
    total = x_transform(place, first, x_tables(length_x, positions(inner)))
    flat = x_transform(place, second, x_tables(length_x, positions(outer)), (total, row_part, col_part))
    tiles = halved // LANES
    return flat.reshape(1, kz_count, tiles, 2, LANES).transpose(0, 1, 3, 2, 4).reshape(1, kz_count, 2, halved)


def solution(mesh):
    return jax.shard_map(
        shards,
        mesh=mesh,
        in_specs=(P(None, "gz", "xy"), P(None, "gz", "xy"), P(None, "gz", "xy"), P()),
        out_specs=P("gz", "xy", None, None),
        check_vma=False,
    )
```

```python
import functools
import math

import jax
import jax.numpy as jnp
import numpy as np
from jax import lax
from jax.experimental import pallas as pl
from jax.experimental.pallas import tpu as pltpu
from jax.sharding import PartitionSpec as P

NX = 2048
NY = 2048
NZ = 2048


SCREEN_WEIGHT = 0.5


def shifted(block, axis, distance):
    devices = range(lax.axis_size(axis))
    route = [(i - distance, i) for i in devices if i - distance in devices]
    return lax.ppermute(block, axis, route)


def cosine_table(length, parity):
    halved = length // 2
    row_index = lax.broadcasted_iota(jnp.int32, (halved, halved), 0)
    col_index = lax.broadcasted_iota(jnp.int32, (halved, halved), 1)
    frequency = 2 * row_index + parity
    phase = frequency * (2 * col_index + 1) % (4 * length)
    scaling = jnp.where(frequency == 0, math.sqrt(1.0 / length), math.sqrt(2.0 / length)).astype(
        jnp.float32
    )
    return scaling * jnp.cos(phase.astype(jnp.float32) * (math.pi / (2 * length)))


def fold_middle(source):
    length = source.shape[1]
    halved = length // 2
    upper_half = source[:, :halved]
    lower_half = lax.rev(source[:, halved:], (1,))
    even_part = jnp.einsum(
        "kq,fql->fkl",
        cosine_table(length, 0),
        upper_half + lower_half,
        precision=lax.Precision.HIGHEST,
    )
    odd_part = jnp.einsum(
        "kq,fql->fkl",
        cosine_table(length, 1),
        upper_half - lower_half,
        precision=lax.Precision.HIGHEST,
    )
    return jnp.stack([even_part, odd_part], axis=2).reshape(source.shape)


def fold_last(source):
    length = source.shape[2]
    halved = length // 2
    upper_half = source[:, :, :halved]
    lower_half = lax.rev(source[:, :, halved:], (2,))
    even_part = jnp.einsum(
        "yzn,mn->yzm",
        upper_half + lower_half,
        cosine_table(length, 0),
        precision=lax.Precision.HIGHEST,
    )
    odd_part = jnp.einsum(
        "yzn,mn->yzm",
        upper_half - lower_half,
        cosine_table(length, 1),
        precision=lax.Precision.HIGHEST,
    )
    return jnp.stack([even_part, odd_part], axis=2)


def eigenvalue(index, length):
    sine = jnp.sin(index.astype(jnp.float32) * (math.pi / (2 * length)))
    return 4.0 * sine * sine


def plain_shards(flux_xface, flux_yspec, flux_zface, frequency_y):
    x_rank = lax.axis_index("xy")
    x_count = lax.axis_size("xy")
    z_rank = lax.axis_index("gz")
    z_count = lax.axis_size("gz")
    planes = flux_xface.shape[1]
    x_width = flux_xface.shape[2]
    x_position = lax.broadcasted_iota(jnp.int32, flux_xface.shape, 2)
    x_keep = jnp.logical_not((x_rank == x_count - 1) & (x_position == x_width - 1))
    masked_x = jnp.where(x_keep, flux_xface, jnp.zeros_like(flux_xface))
    x_edge = shifted(masked_x[:, :, x_width - 1 :], "xy", 1)
    x_before = jnp.concatenate([x_edge, masked_x[:, :, : x_width - 1]], axis=2)
    weight_y = 2.0 * jnp.sin(frequency_y.astype(jnp.float32) * (math.pi / (2 * NY)))
    partial_value = (
        masked_x.astype(jnp.float32)
        - x_before.astype(jnp.float32)
        + weight_y[:, None, None] * flux_yspec.astype(jnp.float32)
    )
    z_position = lax.broadcasted_iota(jnp.int32, flux_zface.shape, 1)
    z_keep = jnp.logical_not((z_rank == z_count - 1) & (z_position == planes - 1))
    masked_z = jnp.where(z_keep, flux_zface, jnp.zeros_like(flux_zface))
    z_edge = shifted(masked_z[:, planes - 1 :, :], "gz", 1)
    z_before = jnp.concatenate([z_edge, masked_z[:, : planes - 1]], axis=1)
    slab = partial_value + masked_z.astype(jnp.float32) - z_before.astype(jnp.float32)
    totals = lax.all_to_all(slab, "gz", split_axis=0, concat_axis=1, tiled=True)
    spectrum_z = fold_middle(totals)
    x_lines = lax.all_to_all(spectrum_z, "xy", split_axis=1, concat_axis=2, tiled=True)
    spectrum = fold_last(x_lines)
    row_count = spectrum.shape[0]
    kz_count = spectrum.shape[1]
    halved = spectrum.shape[3]
    local_freq = lax.dynamic_slice_in_dim(frequency_y, z_rank * row_count, row_count)
    weight_local = 2.0 * jnp.sin(local_freq.astype(jnp.float32) * (math.pi / (2 * NY)))
    kz_index = x_rank * kz_count + lax.broadcasted_iota(jnp.int32, (kz_count,), 0)
    kx_index = 2 * lax.broadcasted_iota(jnp.int32, (2, halved), 1) + lax.broadcasted_iota(
        jnp.int32, (2, halved), 0
    )
    denominator = (
        (weight_local * weight_local)[:, None, None, None]
        + eigenvalue(kz_index, NZ)[None, :, None, None]
        + eigenvalue(kx_index, NX)[None, None, :, :]
        + SCREEN_WEIGHT
    )
    return -spectrum / denominator


LANES = 128
GROUP = 32
META = 16
STEPS = 64.0
TOP = 32700.0
BLOCKS = 8
RESIDUES = 2 * BLOCKS
CUT = 6
SCOPED = 13 << 20


def split_bf16(table):
    high = table.astype(jnp.bfloat16)
    low = (table - high.astype(np.float64)).astype(jnp.bfloat16)
    return np.stack([high, low])


def scaled_cosine(frequency, position, length, wave=np.cos):
    phase = (frequency[:, None] * (2 * position[None, :] + 1)) % (4 * length)
    scaling = np.where(frequency == 0, math.sqrt(1.0 / length), math.sqrt(2.0 / length))
    return scaling[:, None] * wave(phase * (math.pi / (2 * length)))


def z_tables(length):
    inner = np.arange(length // BLOCKS)
    outer = RESIDUES * np.arange(length // RESIDUES)
    pairs = []
    for r in range(1, BLOCKS):
        upper = [scaled_cosine(outer + r, inner, length), -scaled_cosine(outer + r, inner, length, np.sin)]
        mirror = outer + RESIDUES - r
        lower = [scaled_cosine(mirror, inner, length), scaled_cosine(mirror, inner, length, np.sin)]
        pairs.append(np.concatenate([np.concatenate(upper, axis=1), np.concatenate(lower, axis=1)], axis=0))
    ends = [scaled_cosine(outer, inner, length), scaled_cosine(outer + BLOCKS, inner, length)]
    return split_bf16(np.stack(pairs)), split_bf16(np.stack(ends))


def x_tables(length, ranks, width, tiles):
    halved = length // 2
    lanes = np.arange(LANES)
    tables = []
    for p in (0, 1):
        positions = [np.concatenate([j * width + t * LANES + lanes for t in tiles]) for j in range(ranks)]
        tables.append(np.stack([scaled_cosine(2 * np.arange(halved) + p, at, length).T for at in positions]))
    return split_bf16(np.stack(tables))


def lasting(microseconds):
    return pl.CostEstimate(flops=0, bytes_accessed=int(microseconds * 3.69e6), transcendentals=0)


def steps_of(largest):
    return jnp.ceil(jnp.log2(jnp.maximum(largest, 2.0**-100)) * STEPS)


def encoded(values, extra=None):
    largest = jnp.max(jnp.abs(values), axis=1)
    if extra is not None:
        largest = jnp.maximum(largest, extra)
    steps = steps_of(largest)
    factor = TOP * jnp.exp2(steps * (-1.0 / STEPS))
    return jnp.round(values * factor[:, None, :]).astype(jnp.int32), steps, factor


def decoded(codes, steps):
    scale = jnp.exp2(steps * (1.0 / STEPS)) * (1.0 / TOP)
    groups = steps.shape[0]
    values = codes.astype(jnp.int32).astype(jnp.float32).reshape(groups, GROUP, codes.shape[-1])
    return values * scale[:, None, :], scale


def divergence_kernel(tiles, spans, order, has_edge, place, frequency_in, flux_x, flux_y, flux_z, *refs):
    held_x, held_y, held_z, arrived, frequency, frequency_arrived = refs[-6:]
    if len(refs) - 6 < len(order):
        outs = [refs[i // 2].at[i % 2] for i in range(len(order))]
    else:
        outs = refs[: len(order)]
    z_rank, z_count, x_rank, x_count = place[0], place[1], place[2], place[3]
    rows, width = flux_x.shape[1], flux_x.shape[2]
    last_tile = width // LANES - 1
    reverse = x_rank >= x_count // 2
    frequency_copy = pltpu.make_async_copy(frequency_in, frequency, frequency_arrived)
    frequency_copy.start()
    copies = []
    for i, d in enumerate(order):
        y = z_rank ^ d
        for n, (flux, held, (start, stop)) in enumerate(
            ((flux_x, held_x, spans[0]), (flux_y, held_y, spans[1]), (flux_z, held_z, spans[1]))
        ):
            copies.append(pltpu.make_async_copy(flux.at[y, :, start:stop], held.at[i], arrived.at[i, n]))
            copies[-1].start()
    row_at = lax.broadcasted_iota(jnp.int32, (LANES, LANES), 0)
    col_at = lax.broadcasted_iota(jnp.int32, (LANES, LANES), 1)
    col_at = jnp.where(reverse, LANES - 1 - col_at, col_at)
    take = (row_at == col_at).astype(jnp.float32)
    below = (row_at + 1 == col_at).astype(jnp.float32)
    keep = jnp.where((x_rank == x_count - 1) & (row_at == LANES - 1), 0.0, take)
    pick = take.astype(jnp.bfloat16)
    change = (take - below).astype(jnp.bfloat16)
    change_last = (keep - below).astype(jnp.bfloat16)
    wrap = -((row_at == LANES - 1) & (col_at == 0)).astype(jnp.float32)
    wrap = wrap.astype(jnp.bfloat16)
    dot = functools.partial(jnp.dot, preferred_element_type=jnp.float32)
    groups = rows // GROUP
    z_last = jnp.where(z_rank == z_count - 1, rows - 1, rows)
    row_id = lax.broadcasted_iota(jnp.int32, (rows, LANES), 0)
    at_end = lax.broadcasted_iota(jnp.int32, (groups, LANES), 0) == groups - 1
    frequency_copy.wait()
    for i, d in enumerate(order):
        y = z_rank ^ d
        angle = jnp.full((8, LANES), frequency[y], jnp.int32).astype(jnp.float32) * (math.pi / (2 * NY))
        weight = (2.0 * jnp.sin(angle))[:1]
        for n in range(3):
            copies[3 * i + n].wait()
        metas = []
        for at, tile in enumerate(tiles):
            lanes = slice(tile * LANES - spans[1][0], (tile + 1) * LANES - spans[1][0])
            x_lanes = slice(tile * LANES - spans[0][0], (tile + 1) * LANES - spans[0][0])
            value = dot(held_x[i, :, x_lanes], change_last if tile == last_tile else change)
            if tile > 0:
                value += dot(held_x[i, :, x_lanes.start - LANES : x_lanes.start], wrap)
            value += weight * dot(held_y[i, :, lanes], pick)
            face = jnp.where(row_id == z_last, 0.0, dot(held_z[i, :, lanes], pick))
            value += face - jnp.where(row_id == 0, 0.0, pltpu.roll(face, 1, 0))
            halo = -face[rows - 1 :]
            extra = jnp.where(at_end, jnp.abs(halo), 0.0)
            codes, steps, factor = encoded(value.reshape(groups, GROUP, LANES), extra)
            halo_code = jnp.round(halo * factor[groups - 1 :])
            metas.append(jnp.concatenate([steps, halo_code], axis=0))
            spot = pl.ds(pl.multiple_of(jnp.where(reverse, len(tiles) - 1 - at, at) * LANES, LANES), LANES)
            outs[i][:rows, spot] = codes.reshape(rows, LANES).astype(jnp.int16)
        meta = jnp.where(reverse, jnp.concatenate(metas[::-1], axis=1), jnp.concatenate(metas, axis=1))
        filled = [meta]
        if has_edge:
            ending = lax.broadcasted_iota(jnp.int32, (8, LANES), 1) == LANES - 1
            face = lax.dot_general(
                ending.astype(jnp.bfloat16),
                held_x[i, :, (last_tile * LANES - spans[0][0]) :],
                (((1,), (1,)), ((), ())),
                preferred_element_type=jnp.float32,
            )[:1]
            edge_steps = steps_of(jnp.abs(face))
            filled += [jnp.round(face * (TOP * jnp.exp2(edge_steps * (-1.0 / STEPS)))), edge_steps]
        filler = META - groups - len(filled)
        filled.append(jnp.zeros((filler, meta.shape[1]), jnp.float32))
        outs[i][rows:, :] = jnp.concatenate(filled, axis=0).astype(jnp.int32).astype(jnp.int16)


def divergence(tiles, spans, order, place, frequency, fluxes, has_edge, paired=False):
    y_count, rows, width = fluxes[0].shape
    chunk = len(tiles) * LANES
    vmem = pl.BlockSpec(memory_space=pltpu.VMEM)
    operands = [pltpu.with_memory_space_constraint(a, pltpu.HBM) for a in (frequency, *fluxes)]
    widths = [stop - start for start, stop in (spans[0], spans[1], spans[1])]
    scratch = [pltpu.VMEM((len(order), rows, w), jnp.bfloat16) for w in widths]
    scratch += [pltpu.SemaphoreType.DMA((len(order), 3)), pltpu.SMEM((y_count,), jnp.int32), pltpu.SemaphoreType.DMA]
    return pl.pallas_call(
        functools.partial(divergence_kernel, tiles, spans, order, has_edge),
        in_specs=[pl.BlockSpec(memory_space=pltpu.SMEM)] + [pl.BlockSpec(memory_space=pltpu.HBM)] * 4,
        out_specs=[vmem] * (len(order) // 2 if paired else len(order)),
        out_shape=[jax.ShapeDtypeStruct((2, rows + META, chunk), jnp.int16)] * (len(order) // 2)
        if paired
        else [jax.ShapeDtypeStruct((rows + META, chunk), jnp.int16)] * len(order),
        scratch_shapes=scratch,
        compiler_params=pltpu.CompilerParams(vmem_limit_bytes=SCOPED),
        cost_estimate=lasting(1.2 + 0.5 * len(order)),
        name="divergence",
    )(place, *operands)


def part_of(message, row, cut):
    if not isinstance(message, tuple):
        return message, row
    return (message[0], row) if row < cut else (message[1], row - cut)


def z_kernel(gives_edge, place, *refs):
    if gives_edge:
        pieces, refs = refs[:BLOCKS], refs[BLOCKS:]
    else:
        half = BLOCKS // 2
        pieces = [refs[half].at[d // 2] if d % 2 else refs[d // 2].at[0] for d in range(BLOCKS)]
        refs = refs[half + 1 :]
    pair_table, end_table = refs[:2]
    refs = refs[2:]
    if not gives_edge:
        neighbours, refs = refs[:2], refs[2:]
    outs = refs[:-6]
    blocks, halos, edges, high, low, result = refs[-6:]
    z_rank, x_rank = place[0], place[2]
    rows = blocks.shape[1]
    chunk = blocks.shape[2]
    groups = rows // GROUP
    for d in range(BLOCKS):
        source = z_rank ^ d
        meta = pieces[d][rows:, :].astype(jnp.int32).astype(jnp.float32)
        values, scale = decoded(pieces[d][:rows, :], meta[:groups])
        blocks[source] = values.reshape(rows, chunk)
        halos[pl.ds(source, 1), :] = meta[groups : groups + 1] * scale[groups - 1 :]
        if gives_edge:
            edges[pl.ds(source, 1), :] = meta[groups + 1 : groups + 2]
            edges[pl.ds(BLOCKS + source, 1), :] = meta[groups + 2 : groups + 3]
    if not gives_edge:
        beside = jnp.where(x_rank % 2 == 1, *(n[n.shape[0] - META :, :].astype(jnp.int32) for n in neighbours))
        beside = beside.astype(jnp.float32)
        edge = beside[:BLOCKS] * (jnp.exp2(beside[BLOCKS:] * (1.0 / STEPS)) * (1.0 / TOP))
        reverse = x_rank >= place[3] // 2
        spot = pl.ds(pl.multiple_of(jnp.where(reverse, chunk - LANES, 0), LANES), LANES)
        shape = (BLOCKS, LANES)
        column = lax.broadcasted_iota(jnp.int32, shape, 1) == jnp.where(reverse, LANES - 1, 0)
        for b in range(BLOCKS):
            chosen = column & (lax.broadcasted_iota(jnp.int32, shape, 0) == b) & (x_rank > 0)
            blocks[b, :, spot] -= lax.dot_general(
                edge.astype(jnp.bfloat16),
                chosen.astype(jnp.bfloat16),
                (((0,), (0,)), ((), ())),
                preferred_element_type=jnp.float32,
            )
    for b in range(1, BLOCKS):
        blocks[b, :1, :] += halos[b - 1 : b, :]

    near, far, mid = math.cos(math.pi / 8), math.sin(math.pi / 8), math.sqrt(0.5)
    strip = 16

    def keep(r, part, start, value):
        spot = pl.ds(part * rows + start, strip)
        rounded = value.astype(jnp.bfloat16)
        high[r, spot, :] = rounded
        low[r, spot, :] = (value - rounded.astype(jnp.float32)).astype(jnp.bfloat16)

    def combine(i, carry):
        start = pl.multiple_of(i * strip, strip)
        v = [blocks[b, pl.ds(start, strip), :] for b in range(BLOCKS)]
        p1, p2, p3 = v[1] + v[7], v[2] + v[6], v[3] + v[5]
        n1, n2, n3 = v[1] - v[7], v[2] - v[6], v[3] - v[5]
        ends, gap = v[0] + v[4], v[0] - v[4]
        odd = p1 + p3
        even = ends + p2
        keep(0, 0, start, even + odd)
        keep(8, 0, start, even - odd)
        keep(4, 0, start, ends - p2)
        turn = mid * (p1 - p3)
        keep(2, 0, start, gap + turn)
        keep(6, 0, start, gap - turn)
        turn = mid * (n1 + n3)
        keep(2, 1, start, turn + n2)
        keep(6, 1, start, turn - n2)
        keep(4, 1, start, n1 - n3)
        m2 = mid * n2
        s, t = v[0] + m2, near * n1 + far * n3
        keep(1, 0, start, s + t)
        keep(7, 0, start, s - t)
        s, t = v[0] - m2, far * n1 - near * n3
        keep(3, 0, start, s + t)
        keep(5, 0, start, s - t)
        m2 = mid * p2
        s, t = far * p1 + near * p3, m2 + v[4]
        keep(1, 1, start, s + t)
        keep(7, 1, start, s - t)
        s, t = near * p1 - far * p3, m2 - v[4]
        keep(3, 1, start, s + t)
        keep(5, 1, start, s - t)
        return carry

    lax.fori_loop(0, rows // strip, combine, 0)
    dot = functools.partial(jnp.dot, preferred_element_type=jnp.float32)
    half = result.shape[1]
    for r in range(1, BLOCKS):
        value = dot(pair_table[0, r - 1], high[r])
        value += dot(pair_table[0, r - 1], low[r])
        value += dot(pair_table[1, r - 1], high[r])
        result[r] = value[:half]
        result[RESIDUES - r] = value[half:]
    for e, r in enumerate((0, BLOCKS)):
        value = dot(end_table[0, e], high[r, :rows, :])
        value += dot(end_table[0, e], low[r, :rows, :])
        value += dot(end_table[1, e], high[r, :rows, :])
        result[r] = value
    if gives_edge:
        outs = [outs[0], outs[1], (outs[2], outs[4]), outs[3]]
    share = half // len(outs)
    per = share // GROUP
    for e, out in enumerate(outs):
        first = pl.multiple_of((x_rank ^ e) * share, GROUP)
        metas = []
        for r in range(RESIDUES):
            values = result[r, pl.ds(first, share), :].reshape(per, GROUP, chunk)
            codes, steps, _ = encoded(values)
            ref, first_row = part_of(out, r * share, CUT * share)
            ref[first_row : first_row + share, :] = codes.reshape(share, chunk).astype(jnp.int16)
            metas.append(steps)
        if gives_edge and e % 2:
            metas.append(edges[...])
        ref, first_row = part_of(out, RESIDUES * share, CUT * share)
        ref[first_row:, :] = jnp.concatenate(metas, axis=0).astype(jnp.int32).astype(jnp.int16)


def z_transform(place, pieces, tables, x_count, neighbours=()):
    rows = pieces[0].shape[-2] - META
    chunk = pieces[0].shape[-1]
    length = rows * BLOCKS
    out_rows = [length // x_count + (META if neighbours or e % 2 == 0 else 2 * META) for e in range(x_count)]
    if not neighbours:
        share = length // RESIDUES // x_count
        out_rows = [*out_rows[:2], CUT * share, out_rows[3], out_rows[2] - CUT * share]
    vmem = pl.BlockSpec(memory_space=pltpu.VMEM)
    return pl.pallas_call(
        functools.partial(z_kernel, not neighbours),
        in_specs=[pl.BlockSpec(memory_space=pltpu.SMEM)] + [vmem] * (len(pieces) + 2 + len(neighbours)),
        out_specs=[vmem] * len(out_rows),
        out_shape=[jax.ShapeDtypeStruct((r, chunk), jnp.int16) for r in out_rows],
        scratch_shapes=[
            pltpu.VMEM((BLOCKS, rows, chunk), jnp.float32),
            pltpu.VMEM((BLOCKS, chunk), jnp.float32),
            pltpu.VMEM((2 * BLOCKS, chunk), jnp.float32),
            pltpu.VMEM((BLOCKS + 1, 2 * rows, chunk), jnp.bfloat16),
            pltpu.VMEM((BLOCKS + 1, 2 * rows, chunk), jnp.bfloat16),
            pltpu.VMEM((RESIDUES, length // RESIDUES, chunk), jnp.float32),
        ],
        compiler_params=pltpu.CompilerParams(vmem_limit_bytes=SCOPED),
        cost_estimate=lasting(4.2),
        name="z_transform",
    )(place, *pieces, *tables, *neighbours)


def x_kernel(stage, pairs, *refs):
    place = refs[0]
    refs = list(refs[1:])
    pieces = [[refs.pop(0), refs.pop(0)] for _ in pairs]
    if stage == "first":
        pieces[1][1] = (pieces[1][1], refs.pop(0))
    table = refs[0]
    if stage == "first":
        frequency, col_part, out, factor_out, values, high, low = refs[1:]
    elif stage == "last":
        total, factor, out, values, high, low, finished, sent = refs[1:]
    else:
        total, out, values, high, low = refs[1:]
    x_rank, x_count = place[2], 4
    rows, chunk = values.shape[3], values.shape[2] * LANES
    share = rows // RESIDUES
    per = share // GROUP
    lefts = []
    for i, pair in enumerate(pairs):
        for piece, e in zip(pieces[i], pair):
            source = x_rank ^ e
            side = jnp.where(source >= x_count // 2, 1, 0)
            ref, first_row = part_of(piece, rows, CUT * share)
            steps = ref[first_row : first_row + META, :].astype(jnp.int32).astype(jnp.float32)
            for r in range(RESIDUES):
                ref, first_row = part_of(piece, r * share, CUT * share)
                part, _ = decoded(ref[first_row : first_row + share, :], steps[r * per : (r + 1) * per])
                part = part.reshape(share, chunk)
                for t in range(chunk // LANES):
                    values[i, side, t, pl.ds(r, share, stride=RESIDUES), :] = part[:, t * LANES : (t + 1) * LANES]
        left = x_rank ^ pair[0]
        lefts.append(jnp.minimum(left, x_count - 1 - left))
        for t in range(chunk // LANES):
            near, far = values[i, 0, t], values[i, 1, t]
            lanes = slice(t * LANES, (t + 1) * LANES)
            for p, value in enumerate((near + far, near - far)):
                rounded = value.astype(jnp.bfloat16)
                high[i, p, :, lanes] = rounded
                low[i, p, :, lanes] = (value - rounded.astype(jnp.float32)).astype(jnp.bfloat16)
    if stage == "first":
        turn = jnp.full((8, LANES), frequency[place[0]], jnp.int32).astype(jnp.float32)
        sine = jnp.sin(turn * (math.pi / (2 * NY)))[:1]
        kz_index = x_rank * rows + lax.broadcasted_iota(jnp.int32, (rows, LANES), 0)
        row_part = -(4.0 * sine * sine + eigenvalue(kz_index, rows * x_count) + SCREEN_WEIGHT)
    dot = functools.partial(jnp.dot, preferred_element_type=jnp.float32)
    count = table.shape[4]
    width = 256
    per_row = 2 * count // LANES
    bands = 4 if stage == "last" else 1
    band = rows // bands
    for n in range(bands):
        here = slice(n * band, (n + 1) * band)
        for p in range(2):
            for c in range(count // width):
                cols = slice(c * width, (c + 1) * width)
                value = None if stage == "first" else total[p, here, cols]
                for i, left in enumerate(lefts):
                    for data, level in ((high, 0), (low, 0), (high, 1)):
                        term = dot(data[i, p, here, :], table[level, p, left, :, cols])
                        value = term if value is None else value + term
                if stage == "first":
                    below = jnp.concatenate([row_part] * (width // LANES), axis=1) + col_part[p : p + 1, cols]
                    factor_out[p, :, cols] = 1.0 / below
                if stage != "last":
                    out[p, :, cols] = value
                    continue
                value *= factor[p, here, cols]
                for t in range(width // LANES):
                    tile = c * (width // LANES) + t
                    part = value[:, t * LANES : (t + 1) * LANES]
                    finished[n, pl.ds(2 * tile + p, band, stride=per_row), :] = part
        if stage == "last":
            lines = pl.ds(n * band * per_row, band * per_row)
            pltpu.make_async_copy(finished.at[n], out.at[lines], sent.at[n]).start()
    if stage == "last":
        for n in range(bands):
            lines = pl.ds(n * band * per_row, band * per_row)
            pltpu.make_async_copy(finished.at[n], out.at[lines], sent.at[n]).wait()


def x_transform(stage, place, pairs, pieces, table, extra):
    chosen = [pieces[e] for pair in pairs for e in pair]
    rows = chosen[0].shape[0] - META if stage != "last" else chosen[1].shape[0] - META
    if stage == "first":
        chosen.append(pieces[4])
    chunk = chosen[0].shape[1]
    count = table.shape[4]
    vmem = pl.BlockSpec(memory_space=pltpu.VMEM)
    smem = pl.BlockSpec(memory_space=pltpu.SMEM)
    sums = jax.ShapeDtypeStruct((2, rows, count), jnp.float32)
    scratch = [
        pltpu.VMEM((len(pairs), 2, chunk // LANES, rows, LANES), jnp.float32),
        pltpu.VMEM((len(pairs), 2, rows, chunk), jnp.bfloat16),
        pltpu.VMEM((len(pairs), 2, rows, chunk), jnp.bfloat16),
    ]
    out_shape, out_specs = sums, vmem
    if stage == "first":
        out_shape, out_specs = [sums, sums], [vmem, vmem]
    elif stage == "last":
        lines = rows * 2 * count // LANES
        out_shape = jax.ShapeDtypeStruct((lines, LANES), jnp.float32)
        out_specs = pl.BlockSpec(memory_space=pltpu.HBM)
        scratch += [pltpu.VMEM((4, lines // 4, LANES), jnp.float32), pltpu.SemaphoreType.DMA((4,))]
    return pl.pallas_call(
        functools.partial(x_kernel, stage, pairs),
        in_specs=[smem] + [vmem] * (len(chosen) + 1) + ([smem, vmem] if stage == "first" else [vmem] * len(extra)),
        out_specs=out_specs,
        out_shape=out_shape,
        scratch_shapes=scratch,
        compiler_params=pltpu.CompilerParams(vmem_limit_bytes=SCOPED),
        cost_estimate=pl.CostEstimate(
            flops=12 * rows * len(pairs) * chunk * count, bytes_accessed=16 * rows * count, transcendentals=0
        ),
        name="x_transform",
    )(place, *chosen, table, *extra)


def sent(piece, axis, d):
    return lax.ppermute(piece, axis, [(i, i ^ d) for i in range(lax.axis_size(axis))])


def shards(flux_xface, flux_yspec, flux_zface, frequency_y):
    z_count = lax.axis_size("gz")
    x_count = lax.axis_size("xy")
    y_count, planes, x_width = flux_xface.shape
    length_z, length_x = planes * z_count, x_width * x_count
    fits = z_count == BLOCKS and y_count == BLOCKS and x_count == 4 and x_width == 4 * LANES
    if not fits or planes % GROUP or planes // GROUP + 3 > META or planes != 2 * LANES or length_z != RESIDUES * GROUP * x_count:
        return plain_shards(flux_xface, flux_yspec, flux_zface, frequency_y)
    z_rank, x_rank = lax.axis_index("gz"), lax.axis_index("xy")
    place = jnp.stack([z_rank, jnp.int32(z_count), x_rank, jnp.int32(x_count)]).astype(jnp.int32)
    fluxes = (flux_xface, flux_yspec, flux_zface)
    inner, outer = (1, 2), (0, 3)
    whole = (0, x_width)
    inner_spans, outer_spans = (whole, (LANES, 3 * LANES)), (whole, whole)
    tables_z = z_tables(length_z)
    early, late = (6, 7, 2, 4), (3, 5, 1, 0)
    pieces = divergence(inner, inner_spans, early, place, frequency_y, fluxes, True)
    place_later, *pieces = lax.optimization_barrier((place, *pieces))
    first = {d: sent(piece, "gz", d) for d, piece in zip(early, pieces)}
    pieces = divergence(inner, inner_spans, late, place_later, frequency_y, fluxes, True)
    place_later, *pieces = lax.optimization_barrier((place, *pieces))
    first |= {d: sent(piece, "gz", d) if d else piece for d, piece in zip(late, pieces)}
    ahead = divergence(outer, outer_spans, range(BLOCKS), place_later, frequency_y, fluxes, False, True)
    first = z_transform(place, [first[d] for d in range(BLOCKS)], tables_z, x_count)
    ahead, first = lax.optimization_barrier((ahead, first))
    first = {0: first[0], 1: sent(first[1], "xy", 1), 2: sent(first[2], "xy", 2), 3: sent(first[3], "xy", 3), 4: first[4]}
    second = [ahead[0]] + [sent(ahead[u], "gz", 2 * u) for u in (1, 2)]
    last, second[1], first[1] = lax.optimization_barrier((ahead[3], second[1], first[1]))
    second.append(sent(last, "gz", 6))
    second, first[3], first[2] = lax.optimization_barrier((second, first[3], first[2]))
    first[4] = sent(first[4], "xy", 2)
    second.append(sent(jnp.concatenate([a[1:] for a in second], axis=0), "gz", 1))
    second = z_transform(place, second, tables_z, x_count, (first[1], first[3]))
    later = second[2]
    second = {0: second[0]} | {e: sent(second[e], "xy", e) for e in (3, 1)}
    kz_count = length_z // x_count
    halved = length_x // 2
    kx_index = 2 * np.arange(halved)[None, :] + np.arange(2)[:, None]
    col_part = np.asarray(-4.0 * np.sin(kx_index * (math.pi / (2 * length_x))) ** 2, np.float32)
    outside, inside = (0, 3), (1, 2)
    inner_table = x_tables(length_x, x_count // 2, x_width, inner)
    outer_table = x_tables(length_x, x_count // 2, x_width, outer)
    total, factor = x_transform("first", place, (outside, inside), first, inner_table, (frequency_y, col_part))
    later, total = lax.optimization_barrier((later, total))
    second |= {2: sent(later, "xy", 2)}
    total = x_transform("more", place, (outside,), second, outer_table, (total,))
    flat = x_transform("last", place, (inside,), second, outer_table, (total, factor))
    tiles = halved // LANES
    return flat.reshape(1, kz_count, tiles, 2, LANES).transpose(0, 1, 3, 2, 4).reshape(1, kz_count, 2, halved)


def solution(mesh):
    return jax.shard_map(
        shards,
        mesh=mesh,
        in_specs=(P(None, "gz", "xy"), P(None, "gz", "xy"), P(None, "gz", "xy"), P()),
        out_specs=P("gz", "xy", None, None),
        check_vma=False,
    )
```

```python
import functools
import math

import jax
import jax.numpy as jnp
import numpy as np
from jax import lax
from jax.experimental import pallas as pl
from jax.experimental.pallas import tpu as pltpu
from jax.sharding import PartitionSpec as P

NX = 2048
NY = 2048
NZ = 2048


SCREEN_WEIGHT = 0.5


def shifted(block, axis, distance):
    devices = range(lax.axis_size(axis))
    route = [(i - distance, i) for i in devices if i - distance in devices]
    return lax.ppermute(block, axis, route)


def cosine_table(length, parity):
    halved = length // 2
    row_index = lax.broadcasted_iota(jnp.int32, (halved, halved), 0)
    col_index = lax.broadcasted_iota(jnp.int32, (halved, halved), 1)
    frequency = 2 * row_index + parity
    phase = frequency * (2 * col_index + 1) % (4 * length)
    scaling = jnp.where(frequency == 0, math.sqrt(1.0 / length), math.sqrt(2.0 / length)).astype(
        jnp.float32
    )
    return scaling * jnp.cos(phase.astype(jnp.float32) * (math.pi / (2 * length)))


def fold_middle(source):
    length = source.shape[1]
    halved = length // 2
    upper_half = source[:, :halved]
    lower_half = lax.rev(source[:, halved:], (1,))
    even_part = jnp.einsum(
        "kq,fql->fkl",
        cosine_table(length, 0),
        upper_half + lower_half,
        precision=lax.Precision.HIGHEST,
    )
    odd_part = jnp.einsum(
        "kq,fql->fkl",
        cosine_table(length, 1),
        upper_half - lower_half,
        precision=lax.Precision.HIGHEST,
    )
    return jnp.stack([even_part, odd_part], axis=2).reshape(source.shape)


def fold_last(source):
    length = source.shape[2]
    halved = length // 2
    upper_half = source[:, :, :halved]
    lower_half = lax.rev(source[:, :, halved:], (2,))
    even_part = jnp.einsum(
        "yzn,mn->yzm",
        upper_half + lower_half,
        cosine_table(length, 0),
        precision=lax.Precision.HIGHEST,
    )
    odd_part = jnp.einsum(
        "yzn,mn->yzm",
        upper_half - lower_half,
        cosine_table(length, 1),
        precision=lax.Precision.HIGHEST,
    )
    return jnp.stack([even_part, odd_part], axis=2)


def eigenvalue(index, length):
    sine = jnp.sin(index.astype(jnp.float32) * (math.pi / (2 * length)))
    return 4.0 * sine * sine


def plain_shards(flux_xface, flux_yspec, flux_zface, frequency_y):
    x_rank = lax.axis_index("xy")
    x_count = lax.axis_size("xy")
    z_rank = lax.axis_index("gz")
    z_count = lax.axis_size("gz")
    planes = flux_xface.shape[1]
    x_width = flux_xface.shape[2]
    x_position = lax.broadcasted_iota(jnp.int32, flux_xface.shape, 2)
    x_keep = jnp.logical_not((x_rank == x_count - 1) & (x_position == x_width - 1))
    masked_x = jnp.where(x_keep, flux_xface, jnp.zeros_like(flux_xface))
    x_edge = shifted(masked_x[:, :, x_width - 1 :], "xy", 1)
    x_before = jnp.concatenate([x_edge, masked_x[:, :, : x_width - 1]], axis=2)
    weight_y = 2.0 * jnp.sin(frequency_y.astype(jnp.float32) * (math.pi / (2 * NY)))
    partial_value = (
        masked_x.astype(jnp.float32)
        - x_before.astype(jnp.float32)
        + weight_y[:, None, None] * flux_yspec.astype(jnp.float32)
    )
    z_position = lax.broadcasted_iota(jnp.int32, flux_zface.shape, 1)
    z_keep = jnp.logical_not((z_rank == z_count - 1) & (z_position == planes - 1))
    masked_z = jnp.where(z_keep, flux_zface, jnp.zeros_like(flux_zface))
    z_edge = shifted(masked_z[:, planes - 1 :, :], "gz", 1)
    z_before = jnp.concatenate([z_edge, masked_z[:, : planes - 1]], axis=1)
    slab = partial_value + masked_z.astype(jnp.float32) - z_before.astype(jnp.float32)
    totals = lax.all_to_all(slab, "gz", split_axis=0, concat_axis=1, tiled=True)
    spectrum_z = fold_middle(totals)
    x_lines = lax.all_to_all(spectrum_z, "xy", split_axis=1, concat_axis=2, tiled=True)
    spectrum = fold_last(x_lines)
    row_count = spectrum.shape[0]
    kz_count = spectrum.shape[1]
    halved = spectrum.shape[3]
    local_freq = lax.dynamic_slice_in_dim(frequency_y, z_rank * row_count, row_count)
    weight_local = 2.0 * jnp.sin(local_freq.astype(jnp.float32) * (math.pi / (2 * NY)))
    kz_index = x_rank * kz_count + lax.broadcasted_iota(jnp.int32, (kz_count,), 0)
    kx_index = 2 * lax.broadcasted_iota(jnp.int32, (2, halved), 1) + lax.broadcasted_iota(
        jnp.int32, (2, halved), 0
    )
    denominator = (
        (weight_local * weight_local)[:, None, None, None]
        + eigenvalue(kz_index, NZ)[None, :, None, None]
        + eigenvalue(kx_index, NX)[None, None, :, :]
        + SCREEN_WEIGHT
    )
    return -spectrum / denominator


LANES = 128
GROUP = 32
META = 16
STEPS = 64.0
TOP = 32700.0
BLOCKS = 8
RESIDUES = 2 * BLOCKS
CUT = 6
SCOPED = 13 << 20


def split_bf16(table):
    high = table.astype(jnp.bfloat16)
    low = (table - high.astype(np.float64)).astype(jnp.bfloat16)
    return np.stack([high, low])


def scaled_cosine(frequency, position, length, wave=np.cos):
    phase = (frequency[:, None] * (2 * position[None, :] + 1)) % (4 * length)
    scaling = np.where(frequency == 0, math.sqrt(1.0 / length), math.sqrt(2.0 / length))
    return scaling[:, None] * wave(phase * (math.pi / (2 * length)))


def z_tables(length):
    inner = np.arange(length // BLOCKS)
    outer = RESIDUES * np.arange(length // RESIDUES)
    pairs = []
    for r in range(1, BLOCKS):
        upper = [scaled_cosine(outer + r, inner, length), -scaled_cosine(outer + r, inner, length, np.sin)]
        mirror = outer + RESIDUES - r
        lower = [scaled_cosine(mirror, inner, length), scaled_cosine(mirror, inner, length, np.sin)]
        pairs.append(np.concatenate([np.concatenate(upper, axis=1), np.concatenate(lower, axis=1)], axis=0))
    ends = [scaled_cosine(outer, inner, length), scaled_cosine(outer + BLOCKS, inner, length)]
    return split_bf16(np.stack(pairs)), split_bf16(np.stack(ends))


def x_tables(length, ranks, width, tiles):
    halved = length // 2
    lanes = np.arange(LANES)
    tables = []
    for p in (0, 1):
        positions = [np.concatenate([j * width + t * LANES + lanes for t in tiles]) for j in range(ranks)]
        tables.append(np.stack([scaled_cosine(2 * np.arange(halved) + p, at, length).T for at in positions]))
    return split_bf16(np.stack(tables))


def lasting(microseconds):
    return pl.CostEstimate(flops=0, bytes_accessed=int(microseconds * 3.69e6), transcendentals=0)


def steps_of(largest):
    return jnp.ceil(jnp.log2(jnp.maximum(largest, 2.0**-100)) * STEPS)


def encoded(values, extra=None):
    largest = jnp.max(jnp.abs(values), axis=1)
    if extra is not None:
        largest = jnp.maximum(largest, extra)
    steps = steps_of(largest)
    factor = TOP * jnp.exp2(steps * (-1.0 / STEPS))
    return jnp.round(values * factor[:, None, :]).astype(jnp.int32), steps, factor


def decoded(codes, steps):
    scale = jnp.exp2(steps * (1.0 / STEPS)) * (1.0 / TOP)
    groups = steps.shape[0]
    values = codes.astype(jnp.int32).astype(jnp.float32).reshape(groups, GROUP, codes.shape[-1])
    return values * scale[:, None, :], scale


def divergence_kernel(tiles, spans, order, has_edge, place, frequency_in, flux_x, flux_y, flux_z, *refs):
    held_x, held_y, held_z, arrived, frequency, frequency_arrived = refs[-6:]
    if len(refs) - 6 < len(order):
        outs = [refs[i // 2].at[i % 2] for i in range(len(order))]
    else:
        outs = refs[: len(order)]
    z_rank, z_count, x_rank, x_count = place[0], place[1], place[2], place[3]
    rows, width = flux_x.shape[1], flux_x.shape[2]
    last_tile = width // LANES - 1
    reverse = x_rank >= x_count // 2
    frequency_copy = pltpu.make_async_copy(frequency_in, frequency, frequency_arrived)
    frequency_copy.start()
    copies = []
    for i, d in enumerate(order):
        y = z_rank ^ d
        for n, (flux, held, (start, stop)) in enumerate(
            ((flux_x, held_x, spans[0]), (flux_y, held_y, spans[1]), (flux_z, held_z, spans[1]))
        ):
            copies.append(pltpu.make_async_copy(flux.at[y, :, start:stop], held.at[i], arrived.at[i, n]))
            copies[-1].start()
    row_at = lax.broadcasted_iota(jnp.int32, (LANES, LANES), 0)
    col_at = lax.broadcasted_iota(jnp.int32, (LANES, LANES), 1)
    col_at = jnp.where(reverse, LANES - 1 - col_at, col_at)
    take = (row_at == col_at).astype(jnp.float32)
    below = (row_at + 1 == col_at).astype(jnp.float32)
    keep = jnp.where((x_rank == x_count - 1) & (row_at == LANES - 1), 0.0, take)
    pick = take.astype(jnp.bfloat16)
    change = (take - below).astype(jnp.bfloat16)
    change_last = (keep - below).astype(jnp.bfloat16)
    wrap = -((row_at == LANES - 1) & (col_at == 0)).astype(jnp.float32)
    wrap = wrap.astype(jnp.bfloat16)
    dot = functools.partial(jnp.dot, preferred_element_type=jnp.float32)
    groups = rows // GROUP
    z_last = jnp.where(z_rank == z_count - 1, rows - 1, rows)
    row_id = lax.broadcasted_iota(jnp.int32, (rows, LANES), 0)
    at_end = lax.broadcasted_iota(jnp.int32, (groups, LANES), 0) == groups - 1
    frequency_copy.wait()
    for i, d in enumerate(order):
        y = z_rank ^ d
        angle = jnp.full((8, LANES), frequency[y], jnp.int32).astype(jnp.float32) * (math.pi / (2 * NY))
        weight = (2.0 * jnp.sin(angle))[:1]
        for n in range(3):
            copies[3 * i + n].wait()
        metas = []
        for at, tile in enumerate(tiles):
            lanes = slice(tile * LANES - spans[1][0], (tile + 1) * LANES - spans[1][0])
            x_lanes = slice(tile * LANES - spans[0][0], (tile + 1) * LANES - spans[0][0])
            value = dot(held_x[i, :, x_lanes], change_last if tile == last_tile else change)
            if tile > 0:
                value += dot(held_x[i, :, x_lanes.start - LANES : x_lanes.start], wrap)
            value += weight * dot(held_y[i, :, lanes], pick)
            face = jnp.where(row_id == z_last, 0.0, dot(held_z[i, :, lanes], pick))
            value += face - jnp.where(row_id == 0, 0.0, pltpu.roll(face, 1, 0))
            halo = -face[rows - 1 :]
            extra = jnp.where(at_end, jnp.abs(halo), 0.0)
            codes, steps, factor = encoded(value.reshape(groups, GROUP, LANES), extra)
            halo_code = jnp.round(halo * factor[groups - 1 :])
            metas.append(jnp.concatenate([steps, halo_code], axis=0))
            spot = pl.ds(pl.multiple_of(jnp.where(reverse, len(tiles) - 1 - at, at) * LANES, LANES), LANES)
            outs[i][:rows, spot] = codes.reshape(rows, LANES).astype(jnp.int16)
        meta = jnp.where(reverse, jnp.concatenate(metas[::-1], axis=1), jnp.concatenate(metas, axis=1))
        filled = [meta]
        if has_edge:
            ending = lax.broadcasted_iota(jnp.int32, (8, LANES), 1) == LANES - 1
            face = lax.dot_general(
                ending.astype(jnp.bfloat16),
                held_x[i, :, (last_tile * LANES - spans[0][0]) :],
                (((1,), (1,)), ((), ())),
                preferred_element_type=jnp.float32,
            )[:1]
            edge_steps = steps_of(jnp.abs(face))
            filled += [jnp.round(face * (TOP * jnp.exp2(edge_steps * (-1.0 / STEPS)))), edge_steps]
        filler = META - groups - len(filled)
        filled.append(jnp.zeros((filler, meta.shape[1]), jnp.float32))
        outs[i][rows:, :] = jnp.concatenate(filled, axis=0).astype(jnp.int32).astype(jnp.int16)


def divergence(tiles, spans, order, place, frequency, fluxes, has_edge, paired=False):
    y_count, rows, width = fluxes[0].shape
    chunk = len(tiles) * LANES
    vmem = pl.BlockSpec(memory_space=pltpu.VMEM)
    operands = [pltpu.with_memory_space_constraint(a, pltpu.HBM) for a in (frequency, *fluxes)]
    widths = [stop - start for start, stop in (spans[0], spans[1], spans[1])]
    scratch = [pltpu.VMEM((len(order), rows, w), jnp.bfloat16) for w in widths]
    scratch += [pltpu.SemaphoreType.DMA((len(order), 3)), pltpu.SMEM((y_count,), jnp.int32), pltpu.SemaphoreType.DMA]
    return pl.pallas_call(
        functools.partial(divergence_kernel, tiles, spans, order, has_edge),
        in_specs=[pl.BlockSpec(memory_space=pltpu.SMEM)] + [pl.BlockSpec(memory_space=pltpu.HBM)] * 4,
        out_specs=[vmem] * (len(order) // 2 if paired else len(order)),
        out_shape=[jax.ShapeDtypeStruct((2, rows + META, chunk), jnp.int16)] * (len(order) // 2)
        if paired
        else [jax.ShapeDtypeStruct((rows + META, chunk), jnp.int16)] * len(order),
        scratch_shapes=scratch,
        compiler_params=pltpu.CompilerParams(vmem_limit_bytes=SCOPED),
        cost_estimate=lasting(1.2 + 0.5 * len(order)),
        name="divergence",
    )(place, *operands)


def part_of(message, row, cut):
    if not isinstance(message, tuple):
        return message, row
    return (message[0], row) if row < cut else (message[1], row - cut)


def z_kernel(gives_edge, place, *refs):
    if gives_edge:
        pieces, refs = refs[:BLOCKS], refs[BLOCKS:]
    else:
        half = BLOCKS // 2
        pieces = [refs[half].at[d // 2] if d % 2 else refs[d // 2].at[0] for d in range(BLOCKS)]
        refs = refs[half + 1 :]
    pair_table, end_table = refs[:2]
    refs = refs[2:]
    if not gives_edge:
        neighbours, refs = refs[:2], refs[2:]
    outs = refs[:-6]
    blocks, halos, edges, high, low, result = refs[-6:]
    z_rank, x_rank = place[0], place[2]
    rows = blocks.shape[1]
    chunk = blocks.shape[2]
    groups = rows // GROUP
    for d in range(BLOCKS):
        source = z_rank ^ d
        meta = pieces[d][rows:, :].astype(jnp.int32).astype(jnp.float32)
        values, scale = decoded(pieces[d][:rows, :], meta[:groups])
        blocks[source] = values.reshape(rows, chunk)
        halos[pl.ds(source, 1), :] = meta[groups : groups + 1] * scale[groups - 1 :]
        if gives_edge:
            edges[pl.ds(source, 1), :] = meta[groups + 1 : groups + 2]
            edges[pl.ds(BLOCKS + source, 1), :] = meta[groups + 2 : groups + 3]
    if not gives_edge:
        beside = jnp.where(x_rank % 2 == 1, *(n[n.shape[0] - META :, :].astype(jnp.int32) for n in neighbours))
        beside = beside.astype(jnp.float32)
        edge = beside[:BLOCKS] * (jnp.exp2(beside[BLOCKS:] * (1.0 / STEPS)) * (1.0 / TOP))
        reverse = x_rank >= place[3] // 2
        spot = pl.ds(pl.multiple_of(jnp.where(reverse, chunk - LANES, 0), LANES), LANES)
        shape = (BLOCKS, LANES)
        column = lax.broadcasted_iota(jnp.int32, shape, 1) == jnp.where(reverse, LANES - 1, 0)
        for b in range(BLOCKS):
            chosen = column & (lax.broadcasted_iota(jnp.int32, shape, 0) == b) & (x_rank > 0)
            blocks[b, :, spot] -= lax.dot_general(
                edge.astype(jnp.bfloat16),
                chosen.astype(jnp.bfloat16),
                (((0,), (0,)), ((), ())),
                preferred_element_type=jnp.float32,
            )
    for b in range(1, BLOCKS):
        blocks[b, :1, :] += halos[b - 1 : b, :]

    near, far, mid = math.cos(math.pi / 8), math.sin(math.pi / 8), math.sqrt(0.5)
    strip = 16

    def keep(r, part, start, value):
        spot = pl.ds(part * rows + start, strip)
        rounded = value.astype(jnp.bfloat16)
        high[r, spot, :] = rounded
        low[r, spot, :] = (value - rounded.astype(jnp.float32)).astype(jnp.bfloat16)

    def combine(i, carry):
        start = pl.multiple_of(i * strip, strip)
        v = [blocks[b, pl.ds(start, strip), :] for b in range(BLOCKS)]
        p1, p2, p3 = v[1] + v[7], v[2] + v[6], v[3] + v[5]
        n1, n2, n3 = v[1] - v[7], v[2] - v[6], v[3] - v[5]
        ends, gap = v[0] + v[4], v[0] - v[4]
        odd = p1 + p3
        even = ends + p2
        keep(0, 0, start, even + odd)
        keep(8, 0, start, even - odd)
        keep(4, 0, start, ends - p2)
        turn = mid * (p1 - p3)
        keep(2, 0, start, gap + turn)
        keep(6, 0, start, gap - turn)
        turn = mid * (n1 + n3)
        keep(2, 1, start, turn + n2)
        keep(6, 1, start, turn - n2)
        keep(4, 1, start, n1 - n3)
        m2 = mid * n2
        s, t = v[0] + m2, near * n1 + far * n3
        keep(1, 0, start, s + t)
        keep(7, 0, start, s - t)
        s, t = v[0] - m2, far * n1 - near * n3
        keep(3, 0, start, s + t)
        keep(5, 0, start, s - t)
        m2 = mid * p2
        s, t = far * p1 + near * p3, m2 + v[4]
        keep(1, 1, start, s + t)
        keep(7, 1, start, s - t)
        s, t = near * p1 - far * p3, m2 - v[4]
        keep(3, 1, start, s + t)
        keep(5, 1, start, s - t)
        return carry

    lax.fori_loop(0, rows // strip, combine, 0)
    dot = functools.partial(jnp.dot, preferred_element_type=jnp.float32)
    half = result.shape[1]
    for r in range(1, BLOCKS):
        value = dot(pair_table[0, r - 1], high[r])
        value += dot(pair_table[0, r - 1], low[r])
        value += dot(pair_table[1, r - 1], high[r])
        result[r] = value[:half]
        result[RESIDUES - r] = value[half:]
    for e, r in enumerate((0, BLOCKS)):
        value = dot(end_table[0, e], high[r, :rows, :])
        value += dot(end_table[0, e], low[r, :rows, :])
        value += dot(end_table[1, e], high[r, :rows, :])
        result[r] = value
    if gives_edge:
        outs = [outs[0], outs[1], (outs[2], outs[4]), outs[3]]
    share = half // len(outs)
    per = share // GROUP
    for e, out in enumerate(outs):
        first = pl.multiple_of((x_rank ^ e) * share, GROUP)
        metas = []
        for r in range(RESIDUES):
            values = result[r, pl.ds(first, share), :].reshape(per, GROUP, chunk)
            codes, steps, _ = encoded(values)
            ref, first_row = part_of(out, r * share, CUT * share)
            ref[first_row : first_row + share, :] = codes.reshape(share, chunk).astype(jnp.int16)
            metas.append(steps)
        if gives_edge and e % 2:
            metas.append(edges[...])
        ref, first_row = part_of(out, RESIDUES * share, CUT * share)
        ref[first_row:, :] = jnp.concatenate(metas, axis=0).astype(jnp.int32).astype(jnp.int16)


def z_transform(place, pieces, tables, x_count, neighbours=()):
    rows = pieces[0].shape[-2] - META
    chunk = pieces[0].shape[-1]
    length = rows * BLOCKS
    out_rows = [length // x_count + (META if neighbours or e % 2 == 0 else 2 * META) for e in range(x_count)]
    if not neighbours:
        share = length // RESIDUES // x_count
        out_rows = [*out_rows[:2], CUT * share, out_rows[3], out_rows[2] - CUT * share]
    vmem = pl.BlockSpec(memory_space=pltpu.VMEM)
    return pl.pallas_call(
        functools.partial(z_kernel, not neighbours),
        in_specs=[pl.BlockSpec(memory_space=pltpu.SMEM)] + [vmem] * (len(pieces) + 2 + len(neighbours)),
        out_specs=[vmem] * len(out_rows),
        out_shape=[jax.ShapeDtypeStruct((r, chunk), jnp.int16) for r in out_rows],
        scratch_shapes=[
            pltpu.VMEM((BLOCKS, rows, chunk), jnp.float32),
            pltpu.VMEM((BLOCKS, chunk), jnp.float32),
            pltpu.VMEM((2 * BLOCKS, chunk), jnp.float32),
            pltpu.VMEM((BLOCKS + 1, 2 * rows, chunk), jnp.bfloat16),
            pltpu.VMEM((BLOCKS + 1, 2 * rows, chunk), jnp.bfloat16),
            pltpu.VMEM((RESIDUES, length // RESIDUES, chunk), jnp.float32),
        ],
        compiler_params=pltpu.CompilerParams(vmem_limit_bytes=SCOPED),
        cost_estimate=lasting(4.2),
        name="z_transform",
    )(place, *pieces, *tables, *neighbours)


def x_kernel(stage, pairs, halved, *refs):
    place = refs[0]
    refs = list(refs[1:])
    pieces = [[(refs.pop(0), refs.pop(0)) if e in halved else refs.pop(0) for e in pair] for pair in pairs]
    table = refs[0]
    if stage == "first":
        frequency, col_part, out, factor_out, values, high, low = refs[1:]
    elif stage == "last":
        total, factor, out, values, high, low, finished, sent = refs[1:]
    else:
        total, out, values, high, low = refs[1:]
    x_rank, x_count = place[2], 4
    rows, chunk = values.shape[3], values.shape[2] * LANES
    share = rows // RESIDUES
    per = share // GROUP
    lefts = []
    for i, pair in enumerate(pairs):
        for piece, e in zip(pieces[i], pair):
            source = x_rank ^ e
            side = jnp.where(source >= x_count // 2, 1, 0)
            ref, first_row = part_of(piece, rows, CUT * share)
            steps = ref[first_row : first_row + META, :].astype(jnp.int32).astype(jnp.float32)
            for r in range(RESIDUES):
                ref, first_row = part_of(piece, r * share, CUT * share)
                part, _ = decoded(ref[first_row : first_row + share, :], steps[r * per : (r + 1) * per])
                part = part.reshape(share, chunk)
                for t in range(chunk // LANES):
                    values[i, side, t, pl.ds(r, share, stride=RESIDUES), :] = part[:, t * LANES : (t + 1) * LANES]
        left = x_rank ^ pair[0]
        lefts.append(jnp.minimum(left, x_count - 1 - left))
        for t in range(chunk // LANES):
            near, far = values[i, 0, t], values[i, 1, t]
            lanes = slice(t * LANES, (t + 1) * LANES)
            for p, value in enumerate((near + far, near - far)):
                rounded = value.astype(jnp.bfloat16)
                high[i, p, :, lanes] = rounded
                low[i, p, :, lanes] = (value - rounded.astype(jnp.float32)).astype(jnp.bfloat16)
    if stage == "first":
        turn = jnp.full((8, LANES), frequency[place[0]], jnp.int32).astype(jnp.float32)
        sine = jnp.sin(turn * (math.pi / (2 * NY)))[:1]
        kz_index = x_rank * rows + lax.broadcasted_iota(jnp.int32, (rows, LANES), 0)
        row_part = -(4.0 * sine * sine + eigenvalue(kz_index, rows * x_count) + SCREEN_WEIGHT)
    dot = functools.partial(jnp.dot, preferred_element_type=jnp.float32)
    count = table.shape[4]
    width = 256
    per_row = 2 * count // LANES
    bands = 4 if stage == "last" else 1
    band = rows // bands
    for n in range(bands):
        here = slice(n * band, (n + 1) * band)
        for p in range(2):
            for c in range(count // width):
                cols = slice(c * width, (c + 1) * width)
                value = None if stage == "first" else total[p, here, cols]
                for i, left in enumerate(lefts):
                    for data, level in ((high, 0), (low, 0), (high, 1)):
                        term = dot(data[i, p, here, :], table[level, p, left, :, cols])
                        value = term if value is None else value + term
                if stage == "first":
                    below = jnp.concatenate([row_part] * (width // LANES), axis=1) + col_part[p : p + 1, cols]
                    factor_out[p, :, cols] = 1.0 / below
                if stage != "last":
                    out[p, :, cols] = value
                    continue
                value *= factor[p, here, cols]
                for t in range(width // LANES):
                    tile = c * (width // LANES) + t
                    part = value[:, t * LANES : (t + 1) * LANES]
                    finished[n, pl.ds(2 * tile + p, band, stride=per_row), :] = part
        if stage == "last":
            lines = pl.ds(n * band * per_row, band * per_row)
            pltpu.make_async_copy(finished.at[n], out.at[lines], sent.at[n]).start()
    if stage == "last":
        for n in range(bands):
            lines = pl.ds(n * band * per_row, band * per_row)
            pltpu.make_async_copy(finished.at[n], out.at[lines], sent.at[n]).wait()


def x_transform(stage, place, pairs, pieces, table, extra):
    halved = [e for e in pieces if isinstance(pieces[e], tuple)]
    chosen = []
    for pair in pairs:
        for e in pair:
            chosen += pieces[e] if e in halved else [pieces[e]]
    rows = pieces[0].shape[0] - META
    chunk = chosen[0].shape[1]
    count = table.shape[4]
    vmem = pl.BlockSpec(memory_space=pltpu.VMEM)
    smem = pl.BlockSpec(memory_space=pltpu.SMEM)
    sums = jax.ShapeDtypeStruct((2, rows, count), jnp.float32)
    scratch = [
        pltpu.VMEM((len(pairs), 2, chunk // LANES, rows, LANES), jnp.float32),
        pltpu.VMEM((len(pairs), 2, rows, chunk), jnp.bfloat16),
        pltpu.VMEM((len(pairs), 2, rows, chunk), jnp.bfloat16),
    ]
    out_shape, out_specs = sums, vmem
    if stage == "first":
        out_shape, out_specs = [sums, sums], [vmem, vmem]
    elif stage == "last":
        lines = rows * 2 * count // LANES
        out_shape = jax.ShapeDtypeStruct((lines, LANES), jnp.float32)
        out_specs = pl.BlockSpec(memory_space=pltpu.HBM)
        scratch += [pltpu.VMEM((4, lines // 4, LANES), jnp.float32), pltpu.SemaphoreType.DMA((4,))]
    return pl.pallas_call(
        functools.partial(x_kernel, stage, pairs, halved),
        in_specs=[smem] + [vmem] * (len(chosen) + 1) + ([smem, vmem] if stage == "first" else [vmem] * len(extra)),
        out_specs=out_specs,
        out_shape=out_shape,
        scratch_shapes=scratch,
        compiler_params=pltpu.CompilerParams(vmem_limit_bytes=SCOPED),
        cost_estimate=pl.CostEstimate(
            flops=12 * rows * len(pairs) * chunk * count, bytes_accessed=16 * rows * count, transcendentals=0
        ),
        name="x_transform",
    )(place, *chosen, table, *extra)


def sent(piece, axis, d):
    return lax.ppermute(piece, axis, [(i, i ^ d) for i in range(lax.axis_size(axis))])


def shards(flux_xface, flux_yspec, flux_zface, frequency_y):
    z_count = lax.axis_size("gz")
    x_count = lax.axis_size("xy")
    y_count, planes, x_width = flux_xface.shape
    length_z, length_x = planes * z_count, x_width * x_count
    fits = z_count == BLOCKS and y_count == BLOCKS and x_count == 4 and x_width == 4 * LANES
    if not fits or planes % GROUP or planes // GROUP + 3 > META or planes != 2 * LANES or length_z != RESIDUES * GROUP * x_count:
        return plain_shards(flux_xface, flux_yspec, flux_zface, frequency_y)
    z_rank, x_rank = lax.axis_index("gz"), lax.axis_index("xy")
    place = jnp.stack([z_rank, jnp.int32(z_count), x_rank, jnp.int32(x_count)]).astype(jnp.int32)
    fluxes = (flux_xface, flux_yspec, flux_zface)
    inner, outer = (1, 2), (0, 3)
    whole = (0, x_width)
    inner_spans, outer_spans = (whole, (LANES, 3 * LANES)), (whole, whole)
    tables_z = z_tables(length_z)
    early, late = (6, 7, 2, 4), (3, 5, 1, 0)
    pieces = divergence(inner, inner_spans, early, place, frequency_y, fluxes, True)
    place_later, *pieces = lax.optimization_barrier((place, *pieces))
    first = {d: sent(piece, "gz", d) for d, piece in zip(early, pieces)}
    pieces = divergence(inner, inner_spans, late, place_later, frequency_y, fluxes, True)
    place_later, *pieces = lax.optimization_barrier((place, *pieces))
    first |= {d: sent(piece, "gz", d) if d else piece for d, piece in zip(late, pieces)}
    ahead = divergence(outer, outer_spans, range(BLOCKS), place_later, frequency_y, fluxes, False, True)
    ahead, first = lax.optimization_barrier((ahead, first))
    first = z_transform(place, [first[d] for d in range(BLOCKS)], tables_z, x_count)
    first = {0: first[0], 1: sent(first[1], "xy", 1), 2: sent(first[2], "xy", 2), 3: sent(first[3], "xy", 3), 4: first[4]}
    second = [ahead[0]] + [sent(ahead[u], "gz", 2 * u) for u in (1, 2)]
    last = ahead[3]
    second.append(sent(last, "gz", 6))
    second, first[1], first[3], first[2] = lax.optimization_barrier((second, first[1], first[3], first[2]))
    first[4] = sent(first[4], "xy", 2)
    second.append(sent(jnp.concatenate([a[1:] for a in second], axis=0), "gz", 1))
    second = z_transform(place, second, tables_z, x_count, (first[1], first[3]))
    later = second[2]
    second = {0: second[0]} | {e: sent(second[e], "xy", e) for e in (3, 1)}
    kz_count = length_z // x_count
    halved = length_x // 2
    kx_index = 2 * np.arange(halved)[None, :] + np.arange(2)[:, None]
    col_part = np.asarray(-4.0 * np.sin(kx_index * (math.pi / (2 * length_x))) ** 2, np.float32)
    outside, inside = (0, 3), (1, 2)
    inner_table = x_tables(length_x, x_count // 2, x_width, inner)
    outer_table = x_tables(length_x, x_count // 2, x_width, outer)
    first = {0: first[0], 1: first[1], 2: (first[2], first[4]), 3: first[3]}
    total, factor = x_transform("first", place, (outside,), first, inner_table, (frequency_y, col_part))
    later, total = lax.optimization_barrier((later, total))
    second |= {2: sent(later, "xy", 2)}
    total = x_transform("more", place, (inside,), first, inner_table, (total,))
    total = x_transform("more", place, (outside,), second, outer_table, (total,))
    flat = x_transform("last", place, (inside,), second, outer_table, (total, factor))
    tiles = halved // LANES
    return flat.reshape(1, kz_count, tiles, 2, LANES).transpose(0, 1, 3, 2, 4).reshape(1, kz_count, 2, halved)


def solution(mesh):
    return jax.shard_map(
        shards,
        mesh=mesh,
        in_specs=(P(None, "gz", "xy"), P(None, "gz", "xy"), P(None, "gz", "xy"), P()),
        out_specs=P("gz", "xy", None, None),
        check_vma=False,
    )
```

```python
import functools
import math

import jax
import jax.numpy as jnp
import numpy as np
from jax import lax
from jax.experimental import pallas as pl
from jax.experimental.pallas import tpu as pltpu
from jax.sharding import PartitionSpec as P

NX = 2048
NY = 2048
NZ = 2048


SCREEN_WEIGHT = 0.5


def shifted(block, axis, distance):
    devices = range(lax.axis_size(axis))
    route = [(i - distance, i) for i in devices if i - distance in devices]
    return lax.ppermute(block, axis, route)


def cosine_table(length, parity):
    halved = length // 2
    row_index = lax.broadcasted_iota(jnp.int32, (halved, halved), 0)
    col_index = lax.broadcasted_iota(jnp.int32, (halved, halved), 1)
    frequency = 2 * row_index + parity
    phase = frequency * (2 * col_index + 1) % (4 * length)
    scaling = jnp.where(frequency == 0, math.sqrt(1.0 / length), math.sqrt(2.0 / length)).astype(
        jnp.float32
    )
    return scaling * jnp.cos(phase.astype(jnp.float32) * (math.pi / (2 * length)))


def fold_middle(source):
    length = source.shape[1]
    halved = length // 2
    upper_half = source[:, :halved]
    lower_half = lax.rev(source[:, halved:], (1,))
    even_part = jnp.einsum(
        "kq,fql->fkl",
        cosine_table(length, 0),
        upper_half + lower_half,
        precision=lax.Precision.HIGHEST,
    )
    odd_part = jnp.einsum(
        "kq,fql->fkl",
        cosine_table(length, 1),
        upper_half - lower_half,
        precision=lax.Precision.HIGHEST,
    )
    return jnp.stack([even_part, odd_part], axis=2).reshape(source.shape)


def fold_last(source):
    length = source.shape[2]
    halved = length // 2
    upper_half = source[:, :, :halved]
    lower_half = lax.rev(source[:, :, halved:], (2,))
    even_part = jnp.einsum(
        "yzn,mn->yzm",
        upper_half + lower_half,
        cosine_table(length, 0),
        precision=lax.Precision.HIGHEST,
    )
    odd_part = jnp.einsum(
        "yzn,mn->yzm",
        upper_half - lower_half,
        cosine_table(length, 1),
        precision=lax.Precision.HIGHEST,
    )
    return jnp.stack([even_part, odd_part], axis=2)


def eigenvalue(index, length):
    sine = jnp.sin(index.astype(jnp.float32) * (math.pi / (2 * length)))
    return 4.0 * sine * sine


def plain_shards(flux_xface, flux_yspec, flux_zface, frequency_y):
    x_rank = lax.axis_index("xy")
    x_count = lax.axis_size("xy")
    z_rank = lax.axis_index("gz")
    z_count = lax.axis_size("gz")
    planes = flux_xface.shape[1]
    x_width = flux_xface.shape[2]
    x_position = lax.broadcasted_iota(jnp.int32, flux_xface.shape, 2)
    x_keep = jnp.logical_not((x_rank == x_count - 1) & (x_position == x_width - 1))
    masked_x = jnp.where(x_keep, flux_xface, jnp.zeros_like(flux_xface))
    x_edge = shifted(masked_x[:, :, x_width - 1 :], "xy", 1)
    x_before = jnp.concatenate([x_edge, masked_x[:, :, : x_width - 1]], axis=2)
    weight_y = 2.0 * jnp.sin(frequency_y.astype(jnp.float32) * (math.pi / (2 * NY)))
    partial_value = (
        masked_x.astype(jnp.float32)
        - x_before.astype(jnp.float32)
        + weight_y[:, None, None] * flux_yspec.astype(jnp.float32)
    )
    z_position = lax.broadcasted_iota(jnp.int32, flux_zface.shape, 1)
    z_keep = jnp.logical_not((z_rank == z_count - 1) & (z_position == planes - 1))
    masked_z = jnp.where(z_keep, flux_zface, jnp.zeros_like(flux_zface))
    z_edge = shifted(masked_z[:, planes - 1 :, :], "gz", 1)
    z_before = jnp.concatenate([z_edge, masked_z[:, : planes - 1]], axis=1)
    slab = partial_value + masked_z.astype(jnp.float32) - z_before.astype(jnp.float32)
    totals = lax.all_to_all(slab, "gz", split_axis=0, concat_axis=1, tiled=True)
    spectrum_z = fold_middle(totals)
    x_lines = lax.all_to_all(spectrum_z, "xy", split_axis=1, concat_axis=2, tiled=True)
    spectrum = fold_last(x_lines)
    row_count = spectrum.shape[0]
    kz_count = spectrum.shape[1]
    halved = spectrum.shape[3]
    local_freq = lax.dynamic_slice_in_dim(frequency_y, z_rank * row_count, row_count)
    weight_local = 2.0 * jnp.sin(local_freq.astype(jnp.float32) * (math.pi / (2 * NY)))
    kz_index = x_rank * kz_count + lax.broadcasted_iota(jnp.int32, (kz_count,), 0)
    kx_index = 2 * lax.broadcasted_iota(jnp.int32, (2, halved), 1) + lax.broadcasted_iota(
        jnp.int32, (2, halved), 0
    )
    denominator = (
        (weight_local * weight_local)[:, None, None, None]
        + eigenvalue(kz_index, NZ)[None, :, None, None]
        + eigenvalue(kx_index, NX)[None, None, :, :]
        + SCREEN_WEIGHT
    )
    return -spectrum / denominator


LANES = 128
GROUP = 32
META = 16
STEPS = 64.0
TOP = 32700.0
BLOCKS = 8
RESIDUES = 2 * BLOCKS
CUT = 6
SCOPED = 13 << 20


def split_bf16(table):
    high = table.astype(jnp.bfloat16)
    low = (table - high.astype(np.float64)).astype(jnp.bfloat16)
    return np.stack([high, low])


def scaled_cosine(frequency, position, length, wave=np.cos):
    phase = (frequency[:, None] * (2 * position[None, :] + 1)) % (4 * length)
    scaling = np.where(frequency == 0, math.sqrt(1.0 / length), math.sqrt(2.0 / length))
    return scaling[:, None] * wave(phase * (math.pi / (2 * length)))


def z_tables(length):
    inner = np.arange(length // BLOCKS)
    outer = RESIDUES * np.arange(length // RESIDUES)
    pairs = []
    for r in range(1, BLOCKS):
        upper = [scaled_cosine(outer + r, inner, length), -scaled_cosine(outer + r, inner, length, np.sin)]
        mirror = outer + RESIDUES - r
        lower = [scaled_cosine(mirror, inner, length), scaled_cosine(mirror, inner, length, np.sin)]
        pairs.append(np.concatenate([np.concatenate(upper, axis=1), np.concatenate(lower, axis=1)], axis=0))
    ends = [scaled_cosine(outer, inner, length), scaled_cosine(outer + BLOCKS, inner, length)]
    return split_bf16(np.stack(pairs)), split_bf16(np.stack(ends))


def x_tables(length, ranks, width, tiles):
    halved = length // 2
    lanes = np.arange(LANES)
    tables = []
    for p in (0, 1):
        positions = [np.concatenate([j * width + t * LANES + lanes for t in tiles]) for j in range(ranks)]
        tables.append(np.stack([scaled_cosine(2 * np.arange(halved) + p, at, length).T for at in positions]))
    return split_bf16(np.stack(tables))


def lasting(microseconds):
    return pl.CostEstimate(flops=0, bytes_accessed=int(microseconds * 3.69e6), transcendentals=0)


def steps_of(largest):
    return jnp.ceil(jnp.log2(jnp.maximum(largest, 2.0**-100)) * STEPS)


def encoded(values, extra=None):
    largest = jnp.max(jnp.abs(values), axis=1)
    if extra is not None:
        largest = jnp.maximum(largest, extra)
    steps = steps_of(largest)
    factor = TOP * jnp.exp2(steps * (-1.0 / STEPS))
    return jnp.round(values * factor[:, None, :]).astype(jnp.int32), steps, factor


def decoded(codes, steps):
    scale = jnp.exp2(steps * (1.0 / STEPS)) * (1.0 / TOP)
    groups = steps.shape[0]
    values = codes.astype(jnp.int32).astype(jnp.float32).reshape(groups, GROUP, codes.shape[-1])
    return values * scale[:, None, :], scale


def divergence_kernel(tiles, spans, order, has_edge, place, frequency_in, flux_x, flux_y, flux_z, *refs):
    held_x, held_y, held_z, arrived, frequency, frequency_arrived = refs[-6:]
    if len(refs) - 6 < len(order):
        outs = [refs[i // 2].at[i % 2] for i in range(len(order))]
    else:
        outs = refs[: len(order)]
    z_rank, z_count, x_rank, x_count = place[0], place[1], place[2], place[3]
    rows, width = flux_x.shape[1], flux_x.shape[2]
    last_tile = width // LANES - 1
    reverse = x_rank >= x_count // 2
    frequency_copy = pltpu.make_async_copy(frequency_in, frequency, frequency_arrived)
    frequency_copy.start()
    copies = []
    for i, d in enumerate(order):
        y = z_rank ^ d
        for n, (flux, held, (start, stop)) in enumerate(
            ((flux_x, held_x, spans[0]), (flux_y, held_y, spans[1]), (flux_z, held_z, spans[1]))
        ):
            copies.append(pltpu.make_async_copy(flux.at[y, :, start:stop], held.at[i], arrived.at[i, n]))
            copies[-1].start()
    row_at = lax.broadcasted_iota(jnp.int32, (LANES, LANES), 0)
    col_at = lax.broadcasted_iota(jnp.int32, (LANES, LANES), 1)
    col_at = jnp.where(reverse, LANES - 1 - col_at, col_at)
    take = (row_at == col_at).astype(jnp.float32)
    below = (row_at + 1 == col_at).astype(jnp.float32)
    keep = jnp.where((x_rank == x_count - 1) & (row_at == LANES - 1), 0.0, take)
    pick = take.astype(jnp.bfloat16)
    change = (take - below).astype(jnp.bfloat16)
    change_last = (keep - below).astype(jnp.bfloat16)
    wrap = -((row_at == LANES - 1) & (col_at == 0)).astype(jnp.float32)
    wrap = wrap.astype(jnp.bfloat16)
    dot = functools.partial(jnp.dot, preferred_element_type=jnp.float32)
    groups = rows // GROUP
    z_last = jnp.where(z_rank == z_count - 1, rows - 1, rows)
    row_id = lax.broadcasted_iota(jnp.int32, (rows, LANES), 0)
    at_end = lax.broadcasted_iota(jnp.int32, (groups, LANES), 0) == groups - 1
    frequency_copy.wait()
    for i, d in enumerate(order):
        y = z_rank ^ d
        angle = jnp.full((8, LANES), frequency[y], jnp.int32).astype(jnp.float32) * (math.pi / (2 * NY))
        weight = (2.0 * jnp.sin(angle))[:1]
        for n in range(3):
            copies[3 * i + n].wait()
        metas = []
        for at, tile in enumerate(tiles):
            lanes = slice(tile * LANES - spans[1][0], (tile + 1) * LANES - spans[1][0])
            x_lanes = slice(tile * LANES - spans[0][0], (tile + 1) * LANES - spans[0][0])
            value = dot(held_x[i, :, x_lanes], change_last if tile == last_tile else change)
            if tile > 0:
                value += dot(held_x[i, :, x_lanes.start - LANES : x_lanes.start], wrap)
            value += weight * dot(held_y[i, :, lanes], pick)
            face = jnp.where(row_id == z_last, 0.0, dot(held_z[i, :, lanes], pick))
            value += face - jnp.where(row_id == 0, 0.0, pltpu.roll(face, 1, 0))
            halo = -face[rows - 1 :]
            extra = jnp.where(at_end, jnp.abs(halo), 0.0)
            codes, steps, factor = encoded(value.reshape(groups, GROUP, LANES), extra)
            halo_code = jnp.round(halo * factor[groups - 1 :])
            metas.append(jnp.concatenate([steps, halo_code], axis=0))
            spot = pl.ds(pl.multiple_of(jnp.where(reverse, len(tiles) - 1 - at, at) * LANES, LANES), LANES)
            outs[i][:rows, spot] = codes.reshape(rows, LANES).astype(jnp.int16)
        meta = jnp.where(reverse, jnp.concatenate(metas[::-1], axis=1), jnp.concatenate(metas, axis=1))
        filled = [meta]
        if has_edge:
            ending = lax.broadcasted_iota(jnp.int32, (8, LANES), 1) == LANES - 1
            face = lax.dot_general(
                ending.astype(jnp.bfloat16),
                held_x[i, :, (last_tile * LANES - spans[0][0]) :],
                (((1,), (1,)), ((), ())),
                preferred_element_type=jnp.float32,
            )[:1]
            edge_steps = steps_of(jnp.abs(face))
            filled += [jnp.round(face * (TOP * jnp.exp2(edge_steps * (-1.0 / STEPS)))), edge_steps]
        filler = META - groups - len(filled)
        filled.append(jnp.zeros((filler, meta.shape[1]), jnp.float32))
        outs[i][rows:, :] = jnp.concatenate(filled, axis=0).astype(jnp.int32).astype(jnp.int16)


def divergence(tiles, spans, order, place, frequency, fluxes, has_edge, paired=False):
    y_count, rows, width = fluxes[0].shape
    chunk = len(tiles) * LANES
    vmem = pl.BlockSpec(memory_space=pltpu.VMEM)
    operands = [pltpu.with_memory_space_constraint(a, pltpu.HBM) for a in (frequency, *fluxes)]
    widths = [stop - start for start, stop in (spans[0], spans[1], spans[1])]
    scratch = [pltpu.VMEM((len(order), rows, w), jnp.bfloat16) for w in widths]
    scratch += [pltpu.SemaphoreType.DMA((len(order), 3)), pltpu.SMEM((y_count,), jnp.int32), pltpu.SemaphoreType.DMA]
    return pl.pallas_call(
        functools.partial(divergence_kernel, tiles, spans, order, has_edge),
        in_specs=[pl.BlockSpec(memory_space=pltpu.SMEM)] + [pl.BlockSpec(memory_space=pltpu.HBM)] * 4,
        out_specs=[vmem] * (len(order) // 2 if paired else len(order)),
        out_shape=[jax.ShapeDtypeStruct((2, rows + META, chunk), jnp.int16)] * (len(order) // 2)
        if paired
        else [jax.ShapeDtypeStruct((rows + META, chunk), jnp.int16)] * len(order),
        scratch_shapes=scratch,
        compiler_params=pltpu.CompilerParams(vmem_limit_bytes=SCOPED),
        cost_estimate=lasting(1.2 + 0.5 * len(order)),
        name="divergence",
    )(place, *operands)


def part_of(message, row, cut):
    if not isinstance(message, tuple):
        return message, row
    return (message[0], row) if row < cut else (message[1], row - cut)


def z_kernel(gives_edge, place, *refs):
    if gives_edge:
        pieces, refs = refs[:BLOCKS], refs[BLOCKS:]
    else:
        half = BLOCKS // 2
        pieces = [refs[half].at[d // 2] if d % 2 else refs[d // 2].at[0] for d in range(BLOCKS)]
        refs = refs[half + 1 :]
    pair_table, end_table = refs[:2]
    refs = refs[2:]
    if not gives_edge:
        neighbours, refs = refs[:2], refs[2:]
    outs = refs[:-6]
    blocks, halos, edges, high, low, result = refs[-6:]
    z_rank, x_rank = place[0], place[2]
    rows = blocks.shape[1]
    chunk = blocks.shape[2]
    groups = rows // GROUP
    for d in range(BLOCKS):
        source = z_rank ^ d
        meta = pieces[d][rows:, :].astype(jnp.int32).astype(jnp.float32)
        values, scale = decoded(pieces[d][:rows, :], meta[:groups])
        blocks[source] = values.reshape(rows, chunk)
        halos[pl.ds(source, 1), :] = meta[groups : groups + 1] * scale[groups - 1 :]
        if gives_edge:
            edges[pl.ds(source, 1), :] = meta[groups + 1 : groups + 2]
            edges[pl.ds(BLOCKS + source, 1), :] = meta[groups + 2 : groups + 3]
    if not gives_edge:
        beside = jnp.where(x_rank % 2 == 1, *(n[n.shape[0] - META :, :].astype(jnp.int32) for n in neighbours))
        beside = beside.astype(jnp.float32)
        edge = beside[:BLOCKS] * (jnp.exp2(beside[BLOCKS:] * (1.0 / STEPS)) * (1.0 / TOP))
        reverse = x_rank >= place[3] // 2
        spot = pl.ds(pl.multiple_of(jnp.where(reverse, chunk - LANES, 0), LANES), LANES)
        shape = (BLOCKS, LANES)
        column = lax.broadcasted_iota(jnp.int32, shape, 1) == jnp.where(reverse, LANES - 1, 0)
        for b in range(BLOCKS):
            chosen = column & (lax.broadcasted_iota(jnp.int32, shape, 0) == b) & (x_rank > 0)
            blocks[b, :, spot] -= lax.dot_general(
                edge.astype(jnp.bfloat16),
                chosen.astype(jnp.bfloat16),
                (((0,), (0,)), ((), ())),
                preferred_element_type=jnp.float32,
            )
    for b in range(1, BLOCKS):
        blocks[b, :1, :] += halos[b - 1 : b, :]

    near, far, mid = math.cos(math.pi / 8), math.sin(math.pi / 8), math.sqrt(0.5)
    strip = 16

    def keep(r, part, start, value):
        spot = pl.ds(part * rows + start, strip)
        rounded = value.astype(jnp.bfloat16)
        high[r, spot, :] = rounded
        low[r, spot, :] = (value - rounded.astype(jnp.float32)).astype(jnp.bfloat16)

    def combine(i, carry):
        start = pl.multiple_of(i * strip, strip)
        v = [blocks[b, pl.ds(start, strip), :] for b in range(BLOCKS)]
        p1, p2, p3 = v[1] + v[7], v[2] + v[6], v[3] + v[5]
        n1, n2, n3 = v[1] - v[7], v[2] - v[6], v[3] - v[5]
        ends, gap = v[0] + v[4], v[0] - v[4]
        odd = p1 + p3
        even = ends + p2
        keep(0, 0, start, even + odd)
        keep(8, 0, start, even - odd)
        keep(4, 0, start, ends - p2)
        turn = mid * (p1 - p3)
        keep(2, 0, start, gap + turn)
        keep(6, 0, start, gap - turn)
        turn = mid * (n1 + n3)
        keep(2, 1, start, turn + n2)
        keep(6, 1, start, turn - n2)
        keep(4, 1, start, n1 - n3)
        m2 = mid * n2
        s, t = v[0] + m2, near * n1 + far * n3
        keep(1, 0, start, s + t)
        keep(7, 0, start, s - t)
        s, t = v[0] - m2, far * n1 - near * n3
        keep(3, 0, start, s + t)
        keep(5, 0, start, s - t)
        m2 = mid * p2
        s, t = far * p1 + near * p3, m2 + v[4]
        keep(1, 1, start, s + t)
        keep(7, 1, start, s - t)
        s, t = near * p1 - far * p3, m2 - v[4]
        keep(3, 1, start, s + t)
        keep(5, 1, start, s - t)
        return carry

    lax.fori_loop(0, rows // strip, combine, 0)
    dot = functools.partial(jnp.dot, preferred_element_type=jnp.float32)
    half = result.shape[1]
    for r in range(1, BLOCKS):
        value = dot(pair_table[0, r - 1], high[r])
        value += dot(pair_table[0, r - 1], low[r])
        value += dot(pair_table[1, r - 1], high[r])
        result[r] = value[:half]
        result[RESIDUES - r] = value[half:]
    for e, r in enumerate((0, BLOCKS)):
        value = dot(end_table[0, e], high[r, :rows, :])
        value += dot(end_table[0, e], low[r, :rows, :])
        value += dot(end_table[1, e], high[r, :rows, :])
        result[r] = value
    if gives_edge:
        outs = [outs[0], outs[1], (outs[2], outs[4]), outs[3]]
    else:
        last_two, outs = (outs[2], outs[4]), outs[:4]
    share = half // len(outs)
    per = share // GROUP
    for e, out in enumerate(outs):
        first = pl.multiple_of((x_rank ^ e) * share, GROUP)
        metas = []
        for r in range(RESIDUES):
            values = result[r, pl.ds(first, share), :].reshape(per, GROUP, chunk)
            codes, steps, _ = encoded(values)
            ref, first_row = part_of(out, r * share, CUT * share)
            if not gives_edge and e == 2:
                ref, first_row = last_two[r // BLOCKS], r % BLOCKS * share
            ref[first_row : first_row + share, :] = codes.reshape(share, chunk).astype(jnp.int16)
            metas.append(steps)
        if gives_edge and e % 2:
            metas.append(edges[...])
        if not gives_edge and e == 2:
            unused = jnp.zeros((META - BLOCKS, chunk), jnp.float32)
            for n, ref in enumerate(last_two):
                meta = jnp.concatenate([*metas[n * BLOCKS : (n + 1) * BLOCKS], unused], axis=0)
                ref[BLOCKS * share :, :] = meta.astype(jnp.int32).astype(jnp.int16)
            continue
        ref, first_row = part_of(out, RESIDUES * share, CUT * share)
        ref[first_row:, :] = jnp.concatenate(metas, axis=0).astype(jnp.int32).astype(jnp.int16)


def z_transform(place, pieces, tables, x_count, neighbours=()):
    rows = pieces[0].shape[-2] - META
    chunk = pieces[0].shape[-1]
    length = rows * BLOCKS
    out_rows = [length // x_count + (META if neighbours or e % 2 == 0 else 2 * META) for e in range(x_count)]
    if not neighbours:
        share = length // RESIDUES // x_count
        out_rows = [*out_rows[:2], CUT * share, out_rows[3], out_rows[2] - CUT * share]
    else:
        out_rows = [*out_rows[:2], (out_rows[2] + META) // 2, out_rows[3], (out_rows[2] + META) // 2]
    vmem = pl.BlockSpec(memory_space=pltpu.VMEM)
    return pl.pallas_call(
        functools.partial(z_kernel, not neighbours),
        in_specs=[pl.BlockSpec(memory_space=pltpu.SMEM)] + [vmem] * (len(pieces) + 2 + len(neighbours)),
        out_specs=[vmem] * len(out_rows),
        out_shape=[jax.ShapeDtypeStruct((r, chunk), jnp.int16) for r in out_rows],
        scratch_shapes=[
            pltpu.VMEM((BLOCKS, rows, chunk), jnp.float32),
            pltpu.VMEM((BLOCKS, chunk), jnp.float32),
            pltpu.VMEM((2 * BLOCKS, chunk), jnp.float32),
            pltpu.VMEM((BLOCKS + 1, 2 * rows, chunk), jnp.bfloat16),
            pltpu.VMEM((BLOCKS + 1, 2 * rows, chunk), jnp.bfloat16),
            pltpu.VMEM((RESIDUES, length // RESIDUES, chunk), jnp.float32),
        ],
        compiler_params=pltpu.CompilerParams(vmem_limit_bytes=SCOPED),
        cost_estimate=lasting(4.2),
        name="z_transform",
    )(place, *pieces, *tables, *neighbours)


def x_kernel(stage, pairs, halved, side_rows, *refs):
    place = refs[0]
    refs = list(refs[1:])
    pieces = [[(refs.pop(0), refs.pop(0)) if e in halved else refs.pop(0) for e in pair] for pair in pairs]
    table = refs[0]
    if stage == "first":
        frequency, col_part, out, factor_out, values, high, low = refs[1:]
    elif stage == "last":
        total, factor, *refs = refs[1:]
        out, values, high, low, finished, copied = refs[-6:]
    else:
        total, out, values, high, low = refs[1:]
    x_rank, x_count = place[2], 4
    rows, chunk = values.shape[3], values.shape[2] * LANES
    residues = range(RESIDUES) if side_rows is None else range(side_rows * BLOCKS, (side_rows + 1) * BLOCKS)
    share = rows // len(residues)
    per = share // GROUP
    lefts = []
    for i, pair in enumerate(pairs):
        for piece, e in zip(pieces[i], pair):
            source = x_rank ^ e
            side = jnp.where(source >= x_count // 2, 1, 0)
            short = side_rows is not None and e == pair[1]
            ref, first_row = part_of(piece, BLOCKS * share if short else RESIDUES * share, CUT * share)
            steps = ref[first_row : first_row + META, :].astype(jnp.int32).astype(jnp.float32)
            for i_r, r in enumerate(residues):
                at = i_r if short else r
                ref, first_row = part_of(piece, at * share, CUT * share)
                part, _ = decoded(ref[first_row : first_row + share, :], steps[at * per : (at + 1) * per])
                part = part.reshape(share, chunk)
                for t in range(chunk // LANES):
                    start = i_r // BLOCKS * (BLOCKS * share) + i_r % BLOCKS
                    values[i, side, t, pl.ds(start, share, stride=BLOCKS), :] = part[:, t * LANES : (t + 1) * LANES]
        left = x_rank ^ pair[0]
        lefts.append(jnp.minimum(left, x_count - 1 - left))
        for t in range(chunk // LANES):
            near, far = values[i, 0, t], values[i, 1, t]
            lanes = slice(t * LANES, (t + 1) * LANES)
            for p, value in enumerate((near + far, near - far)):
                rounded = value.astype(jnp.bfloat16)
                high[i, p, :, lanes] = rounded
                low[i, p, :, lanes] = (value - rounded.astype(jnp.float32)).astype(jnp.bfloat16)
    if stage == "first":
        turn = jnp.full((8, LANES), frequency[place[0]], jnp.int32).astype(jnp.float32)
        sine = jnp.sin(turn * (math.pi / (2 * NY)))[:1]
        half_row = lax.broadcasted_iota(jnp.int32, (rows // 2, LANES), 0)
        half_kz = x_rank * rows + half_row + BLOCKS * lax.shift_right_logical(half_row, 3)
        kz_index = jnp.concatenate([half_kz, half_kz + BLOCKS], axis=0)
        row_part = -(4.0 * sine * sine + eigenvalue(kz_index, rows * x_count) + SCREEN_WEIGHT)
    dot = functools.partial(jnp.dot, preferred_element_type=jnp.float32)
    count = table.shape[4]
    width = 256
    per_row = 2 * count // LANES
    copies = []
    bands = finished.shape[0] if stage == "last" else 1
    band = rows // bands
    for n in range(bands):
        here = slice(n * band, (n + 1) * band)
        if stage == "last":
            there = slice(side_rows * rows + n * band, side_rows * rows + (n + 1) * band)
        for p in range(2):
            for c in range(count // width):
                cols = slice(c * width, (c + 1) * width)
                value = None if stage == "first" else total[p, there if stage == "last" else here, cols]
                for i, left in enumerate(lefts):
                    for data, level in ((high, 0), (low, 0), (high, 1)):
                        term = dot(data[i, p, here, :], table[level, p, left, :, cols])
                        value = term if value is None else value + term
                if stage == "first":
                    below = jnp.concatenate([row_part] * (width // LANES), axis=1) + col_part[p : p + 1, cols]
                    factor_out[p, :, cols] = 1.0 / below
                if stage != "last":
                    out[p, :, cols] = value
                    continue
                value *= factor[p, there, cols]
                for t in range(width // LANES):
                    tile = c * (width // LANES) + t
                    part = value[:, t * LANES : (t + 1) * LANES]
                    finished[n, pl.ds(2 * tile + p, band, stride=per_row), :] = part
        if stage == "last":
            block = BLOCKS * per_row
            for m in range(band // BLOCKS):
                to = pl.ds((2 * (n * (band // BLOCKS) + m) + side_rows) * block, block)
                source = finished.at[n, pl.ds(m * block, block)]
                copies.append(pltpu.make_async_copy(source, out.at[to], copied.at[len(copies)]))
                copies[-1].start()
    for copy in copies:
        copy.wait()


def x_transform(stage, place, pairs, pieces, table, extra, side_rows=None, written=None):
    halved = [e for e in pieces if isinstance(pieces[e], tuple)]
    chosen = []
    for pair in pairs:
        for e in pair:
            chosen += pieces[e] if e in halved else [pieces[e]]
    rows = pieces[0].shape[0] - META
    line_count = rows * 2 * table.shape[4] // LANES
    aliases = {}
    if stage == "last":
        rows //= 2
    if written is not None:
        extra = (*extra, written)
        aliases = {1 + len(chosen) + 1 + 2: 0}
    chunk = chosen[0].shape[1]
    count = table.shape[4]
    vmem = pl.BlockSpec(memory_space=pltpu.VMEM)
    smem = pl.BlockSpec(memory_space=pltpu.SMEM)
    sums = jax.ShapeDtypeStruct((2, rows, count), jnp.float32)
    scratch = [
        pltpu.VMEM((len(pairs), 2, chunk // LANES, rows, LANES), jnp.float32),
        pltpu.VMEM((len(pairs), 2, rows, chunk), jnp.bfloat16),
        pltpu.VMEM((len(pairs), 2, rows, chunk), jnp.bfloat16),
    ]
    out_shape, out_specs = sums, vmem
    if stage == "first":
        out_shape, out_specs = [sums, sums], [vmem, vmem]
    elif stage == "last":
        out_shape = jax.ShapeDtypeStruct((line_count, LANES), jnp.float32)
        out_specs = pl.BlockSpec(memory_space=pltpu.HBM)
        bands = 2
        scratch += [pltpu.VMEM((bands, line_count // 2 // bands, LANES), jnp.float32)]
        scratch += [pltpu.SemaphoreType.DMA((rows // BLOCKS,))]
    return pl.pallas_call(
        functools.partial(x_kernel, stage, pairs, halved, side_rows),
        in_specs=[smem] + [vmem] * (len(chosen) + 1) + ([smem, vmem] if stage == "first" else [vmem] * min(len(extra), 2) + [out_specs] * len(aliases)),
        out_specs=out_specs,
        out_shape=out_shape,
        input_output_aliases=aliases,
        scratch_shapes=scratch,
        compiler_params=pltpu.CompilerParams(vmem_limit_bytes=SCOPED),
        cost_estimate=pl.CostEstimate(
            flops=12 * rows * len(pairs) * chunk * count, bytes_accessed=16 * rows * count, transcendentals=0
        ),
        name="x_transform",
    )(place, *chosen, table, *extra)


def sent(piece, axis, d):
    return lax.ppermute(piece, axis, [(i, i ^ d) for i in range(lax.axis_size(axis))])


def shards(flux_xface, flux_yspec, flux_zface, frequency_y):
    z_count = lax.axis_size("gz")
    x_count = lax.axis_size("xy")
    y_count, planes, x_width = flux_xface.shape
    length_z, length_x = planes * z_count, x_width * x_count
    fits = z_count == BLOCKS and y_count == BLOCKS and x_count == 4 and x_width == 4 * LANES
    if not fits or planes % GROUP or planes // GROUP + 3 > META or planes != 2 * LANES or length_z != RESIDUES * GROUP * x_count:
        return plain_shards(flux_xface, flux_yspec, flux_zface, frequency_y)
    z_rank, x_rank = lax.axis_index("gz"), lax.axis_index("xy")
    place = jnp.stack([z_rank, jnp.int32(z_count), x_rank, jnp.int32(x_count)]).astype(jnp.int32)
    fluxes = (flux_xface, flux_yspec, flux_zface)
    inner, outer = (1, 2), (0, 3)
    whole = (0, x_width)
    inner_spans, outer_spans = (whole, (LANES, 3 * LANES)), (whole, whole)
    tables_z = z_tables(length_z)
    early, late = (6, 7, 2, 4), (3, 5, 1, 0)
    pieces = divergence(inner, inner_spans, early, place, frequency_y, fluxes, True)
    place_later, *pieces = lax.optimization_barrier((place, *pieces))
    first = {d: sent(piece, "gz", d) for d, piece in zip(early, pieces)}
    pieces = divergence(inner, inner_spans, late, place_later, frequency_y, fluxes, True)
    place_later, *pieces = lax.optimization_barrier((place, *pieces))
    first |= {d: sent(piece, "gz", d) if d else piece for d, piece in zip(late, pieces)}
    ahead = divergence(outer, outer_spans, range(BLOCKS), place_later, frequency_y, fluxes, False, True)
    ahead, first = lax.optimization_barrier((ahead, first))
    first = z_transform(place, [first[d] for d in range(BLOCKS)], tables_z, x_count)
    first = {0: first[0], 1: sent(first[1], "xy", 1), 2: sent(first[2], "xy", 2), 3: sent(first[3], "xy", 3), 4: first[4]}
    second = [ahead[0]] + [sent(ahead[u], "gz", 2 * u) for u in (1, 2)]
    last = ahead[3]
    second.append(sent(last, "gz", 6))
    second, first[1], first[3], first[2] = lax.optimization_barrier((second, first[1], first[3], first[2]))
    first[4] = sent(first[4], "xy", 2)
    second.append(sent(jnp.concatenate([a[1:] for a in second], axis=0), "gz", 1))
    second = z_transform(place, second, tables_z, x_count, (first[1], first[3]))
    later, latest = second[2], second[4]
    second = {0: second[0]} | {e: sent(second[e], "xy", e) for e in (3, 1)}
    kz_count = length_z // x_count
    halved = length_x // 2
    kx_index = 2 * np.arange(halved)[None, :] + np.arange(2)[:, None]
    col_part = np.asarray(-4.0 * np.sin(kx_index * (math.pi / (2 * length_x))) ** 2, np.float32)
    outside, inside = (0, 3), (1, 2)
    inner_table = x_tables(length_x, x_count // 2, x_width, inner)
    outer_table = x_tables(length_x, x_count // 2, x_width, outer)
    first = {0: first[0], 1: first[1], 2: (first[2], first[4]), 3: first[3]}
    total, factor = x_transform("first", place, (outside,), first, inner_table, (frequency_y, col_part))
    later, total = lax.optimization_barrier((later, total))
    second |= {2: sent(later, "xy", 2)}
    total = x_transform("more", place, (inside,), first, inner_table, (total,))
    total = x_transform("more", place, (outside,), second, outer_table, (total,))
    latest, total = lax.optimization_barrier((latest, total))
    latest = sent(latest, "xy", 2)
    flat = x_transform("last", place, (inside,), second, outer_table, (total, factor), 0)
    second[2] = latest
    flat = x_transform("last", place, (inside,), second, outer_table, (total, factor), 1, flat)
    tiles = halved // LANES
    return flat.reshape(1, kz_count, tiles, 2, LANES).transpose(0, 1, 3, 2, 4).reshape(1, kz_count, 2, halved)


def solution(mesh):
    return jax.shard_map(
        shards,
        mesh=mesh,
        in_specs=(P(None, "gz", "xy"), P(None, "gz", "xy"), P(None, "gz", "xy"), P()),
        out_specs=P("gz", "xy", None, None),
        check_vma=False,
    )
```

```python
import functools
import math

import jax
import jax.numpy as jnp
import numpy as np
from jax import lax
from jax.experimental import pallas as pl
from jax.experimental.pallas import tpu as pltpu
from jax.sharding import PartitionSpec as P

NX = 2048
NY = 2048
NZ = 2048


SCREEN_WEIGHT = 0.5


def shifted(block, axis, distance):
    devices = range(lax.axis_size(axis))
    route = [(i - distance, i) for i in devices if i - distance in devices]
    return lax.ppermute(block, axis, route)


def cosine_table(length, parity):
    halved = length // 2
    row_index = lax.broadcasted_iota(jnp.int32, (halved, halved), 0)
    col_index = lax.broadcasted_iota(jnp.int32, (halved, halved), 1)
    frequency = 2 * row_index + parity
    phase = frequency * (2 * col_index + 1) % (4 * length)
    scaling = jnp.where(frequency == 0, math.sqrt(1.0 / length), math.sqrt(2.0 / length)).astype(
        jnp.float32
    )
    return scaling * jnp.cos(phase.astype(jnp.float32) * (math.pi / (2 * length)))


def fold_middle(source):
    length = source.shape[1]
    halved = length // 2
    upper_half = source[:, :halved]
    lower_half = lax.rev(source[:, halved:], (1,))
    even_part = jnp.einsum(
        "kq,fql->fkl",
        cosine_table(length, 0),
        upper_half + lower_half,
        precision=lax.Precision.HIGHEST,
    )
    odd_part = jnp.einsum(
        "kq,fql->fkl",
        cosine_table(length, 1),
        upper_half - lower_half,
        precision=lax.Precision.HIGHEST,
    )
    return jnp.stack([even_part, odd_part], axis=2).reshape(source.shape)


def fold_last(source):
    length = source.shape[2]
    halved = length // 2
    upper_half = source[:, :, :halved]
    lower_half = lax.rev(source[:, :, halved:], (2,))
    even_part = jnp.einsum(
        "yzn,mn->yzm",
        upper_half + lower_half,
        cosine_table(length, 0),
        precision=lax.Precision.HIGHEST,
    )
    odd_part = jnp.einsum(
        "yzn,mn->yzm",
        upper_half - lower_half,
        cosine_table(length, 1),
        precision=lax.Precision.HIGHEST,
    )
    return jnp.stack([even_part, odd_part], axis=2)


def eigenvalue(index, length):
    sine = jnp.sin(index.astype(jnp.float32) * (math.pi / (2 * length)))
    return 4.0 * sine * sine


def plain_shards(flux_xface, flux_yspec, flux_zface, frequency_y):
    x_rank = lax.axis_index("xy")
    x_count = lax.axis_size("xy")
    z_rank = lax.axis_index("gz")
    z_count = lax.axis_size("gz")
    planes = flux_xface.shape[1]
    x_width = flux_xface.shape[2]
    x_position = lax.broadcasted_iota(jnp.int32, flux_xface.shape, 2)
    x_keep = jnp.logical_not((x_rank == x_count - 1) & (x_position == x_width - 1))
    masked_x = jnp.where(x_keep, flux_xface, jnp.zeros_like(flux_xface))
    x_edge = shifted(masked_x[:, :, x_width - 1 :], "xy", 1)
    x_before = jnp.concatenate([x_edge, masked_x[:, :, : x_width - 1]], axis=2)
    weight_y = 2.0 * jnp.sin(frequency_y.astype(jnp.float32) * (math.pi / (2 * NY)))
    partial_value = (
        masked_x.astype(jnp.float32)
        - x_before.astype(jnp.float32)
        + weight_y[:, None, None] * flux_yspec.astype(jnp.float32)
    )
    z_position = lax.broadcasted_iota(jnp.int32, flux_zface.shape, 1)
    z_keep = jnp.logical_not((z_rank == z_count - 1) & (z_position == planes - 1))
    masked_z = jnp.where(z_keep, flux_zface, jnp.zeros_like(flux_zface))
    z_edge = shifted(masked_z[:, planes - 1 :, :], "gz", 1)
    z_before = jnp.concatenate([z_edge, masked_z[:, : planes - 1]], axis=1)
    slab = partial_value + masked_z.astype(jnp.float32) - z_before.astype(jnp.float32)
    totals = lax.all_to_all(slab, "gz", split_axis=0, concat_axis=1, tiled=True)
    spectrum_z = fold_middle(totals)
    x_lines = lax.all_to_all(spectrum_z, "xy", split_axis=1, concat_axis=2, tiled=True)
    spectrum = fold_last(x_lines)
    row_count = spectrum.shape[0]
    kz_count = spectrum.shape[1]
    halved = spectrum.shape[3]
    local_freq = lax.dynamic_slice_in_dim(frequency_y, z_rank * row_count, row_count)
    weight_local = 2.0 * jnp.sin(local_freq.astype(jnp.float32) * (math.pi / (2 * NY)))
    kz_index = x_rank * kz_count + lax.broadcasted_iota(jnp.int32, (kz_count,), 0)
    kx_index = 2 * lax.broadcasted_iota(jnp.int32, (2, halved), 1) + lax.broadcasted_iota(
        jnp.int32, (2, halved), 0
    )
    denominator = (
        (weight_local * weight_local)[:, None, None, None]
        + eigenvalue(kz_index, NZ)[None, :, None, None]
        + eigenvalue(kx_index, NX)[None, None, :, :]
        + SCREEN_WEIGHT
    )
    return -spectrum / denominator


LANES = 128
GROUP = 32
META = 16
STEPS = 64.0
TOP = 32700.0
BLOCKS = 8
RESIDUES = 2 * BLOCKS
CUT = 6
SCOPED = 13 << 20


def split_bf16(table):
    high = table.astype(jnp.bfloat16)
    low = (table - high.astype(np.float64)).astype(jnp.bfloat16)
    return np.stack([high, low])


def scaled_cosine(frequency, position, length, wave=np.cos):
    phase = (frequency[:, None] * (2 * position[None, :] + 1)) % (4 * length)
    scaling = np.where(frequency == 0, math.sqrt(1.0 / length), math.sqrt(2.0 / length))
    return scaling[:, None] * wave(phase * (math.pi / (2 * length)))


def z_tables(length):
    inner = np.arange(length // BLOCKS)
    outer = RESIDUES * np.arange(length // RESIDUES)
    pairs = []
    for r in range(1, BLOCKS):
        upper = [scaled_cosine(outer + r, inner, length), -scaled_cosine(outer + r, inner, length, np.sin)]
        mirror = outer + RESIDUES - r
        lower = [scaled_cosine(mirror, inner, length), scaled_cosine(mirror, inner, length, np.sin)]
        pairs.append(np.concatenate([np.concatenate(upper, axis=1), np.concatenate(lower, axis=1)], axis=0))
    ends = [scaled_cosine(outer, inner, length), scaled_cosine(outer + BLOCKS, inner, length)]
    return split_bf16(np.stack(pairs)), split_bf16(np.stack(ends))


def x_tables(length, ranks, width, tiles):
    halved = length // 2
    lanes = np.arange(LANES)
    tables = []
    for p in (0, 1):
        positions = [np.concatenate([j * width + t * LANES + lanes for t in tiles]) for j in range(ranks)]
        tables.append(np.stack([scaled_cosine(2 * np.arange(halved) + p, at, length).T for at in positions]))
    return split_bf16(np.stack(tables))


def lasting(microseconds):
    return pl.CostEstimate(flops=0, bytes_accessed=int(microseconds * 3.69e6), transcendentals=0)


def steps_of(largest):
    return jnp.ceil(jnp.log2(jnp.maximum(largest, 2.0**-100)) * STEPS)


def encoded(values, extra=None):
    largest = jnp.max(jnp.abs(values), axis=1)
    if extra is not None:
        largest = jnp.maximum(largest, extra)
    steps = steps_of(largest)
    factor = TOP * jnp.exp2(steps * (-1.0 / STEPS))
    return jnp.round(values * factor[:, None, :]).astype(jnp.int32), steps, factor


def decoded(codes, steps):
    scale = jnp.exp2(steps * (1.0 / STEPS)) * (1.0 / TOP)
    groups = steps.shape[0]
    values = codes.astype(jnp.int32).astype(jnp.float32).reshape(groups, GROUP, codes.shape[-1])
    return values * scale[:, None, :], scale


def divergence_kernel(tiles, spans, order, has_edge, place, frequency_in, flux_x, flux_y, flux_z, *refs):
    held_x, held_y, held_z, arrived, frequency, frequency_arrived = refs[-6:]
    if len(refs) - 6 < len(order):
        outs = [refs[i // 2].at[i % 2] for i in range(len(order))]
    else:
        outs = refs[: len(order)]
    z_rank, z_count, x_rank, x_count = place[0], place[1], place[2], place[3]
    rows, width = flux_x.shape[1], flux_x.shape[2]
    last_tile = width // LANES - 1
    reverse = x_rank >= x_count // 2
    frequency_copy = pltpu.make_async_copy(frequency_in, frequency, frequency_arrived)
    frequency_copy.start()
    copies = []
    for i, d in enumerate(order):
        y = z_rank ^ d
        for n, (flux, held, (start, stop)) in enumerate(
            ((flux_x, held_x, spans[0]), (flux_y, held_y, spans[1]), (flux_z, held_z, spans[1]))
        ):
            copies.append(pltpu.make_async_copy(flux.at[y, :, start:stop], held.at[i], arrived.at[i, n]))
            copies[-1].start()
    row_at = lax.broadcasted_iota(jnp.int32, (LANES, LANES), 0)
    col_at = lax.broadcasted_iota(jnp.int32, (LANES, LANES), 1)
    col_at = jnp.where(reverse, LANES - 1 - col_at, col_at)
    take = (row_at == col_at).astype(jnp.float32)
    below = (row_at + 1 == col_at).astype(jnp.float32)
    keep = jnp.where((x_rank == x_count - 1) & (row_at == LANES - 1), 0.0, take)
    pick = take.astype(jnp.bfloat16)
    change = (take - below).astype(jnp.bfloat16)
    change_last = (keep - below).astype(jnp.bfloat16)
    wrap = -((row_at == LANES - 1) & (col_at == 0)).astype(jnp.float32)
    wrap = wrap.astype(jnp.bfloat16)
    dot = functools.partial(jnp.dot, preferred_element_type=jnp.float32)
    groups = rows // GROUP
    z_last = jnp.where(z_rank == z_count - 1, rows - 1, rows)
    row_id = lax.broadcasted_iota(jnp.int32, (rows, LANES), 0)
    at_end = lax.broadcasted_iota(jnp.int32, (groups, LANES), 0) == groups - 1
    frequency_copy.wait()
    for i, d in enumerate(order):
        y = z_rank ^ d
        angle = jnp.full((8, LANES), frequency[y], jnp.int32).astype(jnp.float32) * (math.pi / (2 * NY))
        weight = (2.0 * jnp.sin(angle))[:1]
        for n in range(3):
            copies[3 * i + n].wait()
        metas = []
        for at, tile in enumerate(tiles):
            lanes = slice(tile * LANES - spans[1][0], (tile + 1) * LANES - spans[1][0])
            x_lanes = slice(tile * LANES - spans[0][0], (tile + 1) * LANES - spans[0][0])
            value = dot(held_x[i, :, x_lanes], change_last if tile == last_tile else change)
            if tile > 0:
                value += dot(held_x[i, :, x_lanes.start - LANES : x_lanes.start], wrap)
            value += weight * dot(held_y[i, :, lanes], pick)
            face = jnp.where(row_id == z_last, 0.0, dot(held_z[i, :, lanes], pick))
            value += face - jnp.where(row_id == 0, 0.0, pltpu.roll(face, 1, 0))
            halo = -face[rows - 1 :]
            extra = jnp.where(at_end, jnp.abs(halo), 0.0)
            codes, steps, factor = encoded(value.reshape(groups, GROUP, LANES), extra)
            halo_code = jnp.round(halo * factor[groups - 1 :])
            metas.append(jnp.concatenate([steps, halo_code], axis=0))
            spot = pl.ds(pl.multiple_of(jnp.where(reverse, len(tiles) - 1 - at, at) * LANES, LANES), LANES)
            outs[i][:rows, spot] = codes.reshape(rows, LANES).astype(jnp.int16)
        meta = jnp.where(reverse, jnp.concatenate(metas[::-1], axis=1), jnp.concatenate(metas, axis=1))
        filled = [meta]
        if has_edge:
            ending = lax.broadcasted_iota(jnp.int32, (8, LANES), 1) == LANES - 1
            face = lax.dot_general(
                ending.astype(jnp.bfloat16),
                held_x[i, :, (last_tile * LANES - spans[0][0]) :],
                (((1,), (1,)), ((), ())),
                preferred_element_type=jnp.float32,
            )[:1]
            edge_steps = steps_of(jnp.abs(face))
            filled += [jnp.round(face * (TOP * jnp.exp2(edge_steps * (-1.0 / STEPS)))), edge_steps]
        filler = META - groups - len(filled)
        filled.append(jnp.zeros((filler, meta.shape[1]), jnp.float32))
        outs[i][rows:, :] = jnp.concatenate(filled, axis=0).astype(jnp.int32).astype(jnp.int16)


def divergence(tiles, spans, order, place, frequency, fluxes, has_edge, paired=False):
    y_count, rows, width = fluxes[0].shape
    chunk = len(tiles) * LANES
    vmem = pl.BlockSpec(memory_space=pltpu.VMEM)
    operands = [pltpu.with_memory_space_constraint(a, pltpu.HBM) for a in (frequency, *fluxes)]
    widths = [stop - start for start, stop in (spans[0], spans[1], spans[1])]
    scratch = [pltpu.VMEM((len(order), rows, w), jnp.bfloat16) for w in widths]
    scratch += [pltpu.SemaphoreType.DMA((len(order), 3)), pltpu.SMEM((y_count,), jnp.int32), pltpu.SemaphoreType.DMA]
    return pl.pallas_call(
        functools.partial(divergence_kernel, tiles, spans, order, has_edge),
        in_specs=[pl.BlockSpec(memory_space=pltpu.SMEM)] + [pl.BlockSpec(memory_space=pltpu.HBM)] * 4,
        out_specs=[vmem] * (len(order) // 2 if paired else len(order)),
        out_shape=[jax.ShapeDtypeStruct((2, rows + META, chunk), jnp.int16)] * (len(order) // 2)
        if paired
        else [jax.ShapeDtypeStruct((rows + META, chunk), jnp.int16)] * len(order),
        scratch_shapes=scratch,
        compiler_params=pltpu.CompilerParams(vmem_limit_bytes=SCOPED),
        cost_estimate=lasting(1.2 + 0.5 * len(order)),
        name="divergence",
    )(place, *operands)


def part_of(message, row, cut):
    if not isinstance(message, tuple):
        return message, row
    return (message[0], row) if row < cut else (message[1], row - cut)


def z_kernel(gives_edge, place, *refs):
    if gives_edge:
        pieces, refs = refs[:BLOCKS], refs[BLOCKS:]
    else:
        half = BLOCKS // 2
        pieces = [refs[half].at[d // 2] if d % 2 else refs[d // 2].at[0] for d in range(BLOCKS)]
        refs = refs[half + 1 :]
    pair_table, end_table = refs[:2]
    refs = refs[2:]
    if not gives_edge:
        neighbours, refs = refs[:2], refs[2:]
    outs = refs[:-6]
    blocks, halos, edges, high, low, result = refs[-6:]
    z_rank, x_rank = place[0], place[2]
    rows = blocks.shape[1]
    chunk = blocks.shape[2]
    groups = rows // GROUP
    for d in range(BLOCKS):
        source = z_rank ^ d
        meta = pieces[d][rows:, :].astype(jnp.int32).astype(jnp.float32)
        values, scale = decoded(pieces[d][:rows, :], meta[:groups])
        blocks[source] = values.reshape(rows, chunk)
        halos[pl.ds(source, 1), :] = meta[groups : groups + 1] * scale[groups - 1 :]
        if gives_edge:
            edges[pl.ds(source, 1), :] = meta[groups + 1 : groups + 2]
            edges[pl.ds(BLOCKS + source, 1), :] = meta[groups + 2 : groups + 3]
    if not gives_edge:
        beside = jnp.where(x_rank % 2 == 1, *(n[n.shape[0] - META :, :].astype(jnp.int32) for n in neighbours))
        beside = beside.astype(jnp.float32)
        edge = beside[:BLOCKS] * (jnp.exp2(beside[BLOCKS:] * (1.0 / STEPS)) * (1.0 / TOP))
        reverse = x_rank >= place[3] // 2
        spot = pl.ds(pl.multiple_of(jnp.where(reverse, chunk - LANES, 0), LANES), LANES)
        shape = (BLOCKS, LANES)
        column = lax.broadcasted_iota(jnp.int32, shape, 1) == jnp.where(reverse, LANES - 1, 0)
        for b in range(BLOCKS):
            chosen = column & (lax.broadcasted_iota(jnp.int32, shape, 0) == b) & (x_rank > 0)
            blocks[b, :, spot] -= lax.dot_general(
                edge.astype(jnp.bfloat16),
                chosen.astype(jnp.bfloat16),
                (((0,), (0,)), ((), ())),
                preferred_element_type=jnp.float32,
            )
    for b in range(1, BLOCKS):
        blocks[b, :1, :] += halos[b - 1 : b, :]

    near, far, mid = math.cos(math.pi / 8), math.sin(math.pi / 8), math.sqrt(0.5)
    strip = 16

    def keep(r, part, start, value):
        spot = pl.ds(part * rows + start, strip)
        rounded = value.astype(jnp.bfloat16)
        high[r, spot, :] = rounded
        low[r, spot, :] = (value - rounded.astype(jnp.float32)).astype(jnp.bfloat16)

    def combine(i, carry):
        start = pl.multiple_of(i * strip, strip)
        v = [blocks[b, pl.ds(start, strip), :] for b in range(BLOCKS)]
        p1, p2, p3 = v[1] + v[7], v[2] + v[6], v[3] + v[5]
        n1, n2, n3 = v[1] - v[7], v[2] - v[6], v[3] - v[5]
        ends, gap = v[0] + v[4], v[0] - v[4]
        odd = p1 + p3
        even = ends + p2
        keep(0, 0, start, even + odd)
        keep(8, 0, start, even - odd)
        keep(4, 0, start, ends - p2)
        turn = mid * (p1 - p3)
        keep(2, 0, start, gap + turn)
        keep(6, 0, start, gap - turn)
        turn = mid * (n1 + n3)
        keep(2, 1, start, turn + n2)
        keep(6, 1, start, turn - n2)
        keep(4, 1, start, n1 - n3)
        m2 = mid * n2
        s, t = v[0] + m2, near * n1 + far * n3
        keep(1, 0, start, s + t)
        keep(7, 0, start, s - t)
        s, t = v[0] - m2, far * n1 - near * n3
        keep(3, 0, start, s + t)
        keep(5, 0, start, s - t)
        m2 = mid * p2
        s, t = far * p1 + near * p3, m2 + v[4]
        keep(1, 1, start, s + t)
        keep(7, 1, start, s - t)
        s, t = near * p1 - far * p3, m2 - v[4]
        keep(3, 1, start, s + t)
        keep(5, 1, start, s - t)
        return carry

    lax.fori_loop(0, rows // strip, combine, 0, unroll=4)
    dot = functools.partial(jnp.dot, preferred_element_type=jnp.float32)
    half = result.shape[1]
    for r in range(1, BLOCKS):
        value = dot(pair_table[0, r - 1], high[r])
        value += dot(pair_table[0, r - 1], low[r])
        value += dot(pair_table[1, r - 1], high[r])
        result[r] = value[:half]
        result[RESIDUES - r] = value[half:]
    for e, r in enumerate((0, BLOCKS)):
        value = dot(end_table[0, e], high[r, :rows, :])
        value += dot(end_table[0, e], low[r, :rows, :])
        value += dot(end_table[1, e], high[r, :rows, :])
        result[r] = value
    if gives_edge:
        outs = [outs[0], outs[1], (outs[2], outs[4]), outs[3]]
    else:
        last_two, outs = (outs[2], outs[4]), outs[:4]
    share = half // len(outs)
    per = share // GROUP
    for e, out in enumerate(outs):
        first = pl.multiple_of((x_rank ^ e) * share, GROUP)
        metas = []
        for r in range(RESIDUES):
            values = result[r, pl.ds(first, share), :].reshape(per, GROUP, chunk)
            codes, steps, _ = encoded(values)
            ref, first_row = part_of(out, r * share, CUT * share)
            if not gives_edge and e == 2:
                ref, first_row = last_two[r // BLOCKS], r % BLOCKS * share
            ref[first_row : first_row + share, :] = codes.reshape(share, chunk).astype(jnp.int16)
            metas.append(steps)
        if gives_edge and e % 2:
            metas.append(edges[...])
        if not gives_edge and e == 2:
            unused = jnp.zeros((META - BLOCKS, chunk), jnp.float32)
            for n, ref in enumerate(last_two):
                meta = jnp.concatenate([*metas[n * BLOCKS : (n + 1) * BLOCKS], unused], axis=0)
                ref[BLOCKS * share :, :] = meta.astype(jnp.int32).astype(jnp.int16)
            continue
        ref, first_row = part_of(out, RESIDUES * share, CUT * share)
        ref[first_row:, :] = jnp.concatenate(metas, axis=0).astype(jnp.int32).astype(jnp.int16)


def z_transform(place, pieces, tables, x_count, neighbours=()):
    rows = pieces[0].shape[-2] - META
    chunk = pieces[0].shape[-1]
    length = rows * BLOCKS
    out_rows = [length // x_count + (META if neighbours or e % 2 == 0 else 2 * META) for e in range(x_count)]
    if not neighbours:
        share = length // RESIDUES // x_count
        out_rows = [*out_rows[:2], CUT * share, out_rows[3], out_rows[2] - CUT * share]
    else:
        out_rows = [*out_rows[:2], (out_rows[2] + META) // 2, out_rows[3], (out_rows[2] + META) // 2]
    vmem = pl.BlockSpec(memory_space=pltpu.VMEM)
    return pl.pallas_call(
        functools.partial(z_kernel, not neighbours),
        in_specs=[pl.BlockSpec(memory_space=pltpu.SMEM)] + [vmem] * (len(pieces) + 2 + len(neighbours)),
        out_specs=[vmem] * len(out_rows),
        out_shape=[jax.ShapeDtypeStruct((r, chunk), jnp.int16) for r in out_rows],
        scratch_shapes=[
            pltpu.VMEM((BLOCKS, rows, chunk), jnp.float32),
            pltpu.VMEM((BLOCKS, chunk), jnp.float32),
            pltpu.VMEM((2 * BLOCKS, chunk), jnp.float32),
            pltpu.VMEM((BLOCKS + 1, 2 * rows, chunk), jnp.bfloat16),
            pltpu.VMEM((BLOCKS + 1, 2 * rows, chunk), jnp.bfloat16),
            pltpu.VMEM((RESIDUES, length // RESIDUES, chunk), jnp.float32),
        ],
        compiler_params=pltpu.CompilerParams(vmem_limit_bytes=SCOPED),
        cost_estimate=lasting(4.2),
        name="z_transform",
    )(place, *pieces, *tables, *neighbours)


def x_kernel(stage, pairs, halved, side_rows, *refs):
    place = refs[0]
    refs = list(refs[1:])
    pieces = [[(refs.pop(0), refs.pop(0)) if e in halved else refs.pop(0) for e in pair] for pair in pairs]
    table = refs[0]
    if stage == "first":
        frequency, col_part, out, factor_out, values, high, low = refs[1:]
    elif stage == "last":
        total, factor, *refs = refs[1:]
        out, values, high, low, finished, copied = refs[-6:]
    else:
        total, out, values, high, low = refs[1:]
    x_rank, x_count = place[2], 4
    rows, chunk = values.shape[3], values.shape[2] * LANES
    residues = range(RESIDUES) if side_rows is None else range(side_rows * BLOCKS, (side_rows + 1) * BLOCKS)
    share = rows // len(residues)
    per = share // GROUP
    lefts = []
    for i, pair in enumerate(pairs):
        for piece, e in zip(pieces[i], pair):
            source = x_rank ^ e
            side = jnp.where(source >= x_count // 2, 1, 0)
            short = side_rows is not None and e == pair[1]
            ref, first_row = part_of(piece, BLOCKS * share if short else RESIDUES * share, CUT * share)
            steps = ref[first_row : first_row + META, :].astype(jnp.int32).astype(jnp.float32)
            for i_r, r in enumerate(residues):
                at = i_r if short else r
                ref, first_row = part_of(piece, at * share, CUT * share)
                part, _ = decoded(ref[first_row : first_row + share, :], steps[at * per : (at + 1) * per])
                part = part.reshape(share, chunk)
                for t in range(chunk // LANES):
                    start = i_r // BLOCKS * (BLOCKS * share) + i_r % BLOCKS
                    values[i, side, t, pl.ds(start, share, stride=BLOCKS), :] = part[:, t * LANES : (t + 1) * LANES]
        left = x_rank ^ pair[0]
        lefts.append(jnp.minimum(left, x_count - 1 - left))
        for t in range(chunk // LANES):
            near, far = values[i, 0, t], values[i, 1, t]
            lanes = slice(t * LANES, (t + 1) * LANES)
            for p, value in enumerate((near + far, near - far)):
                rounded = value.astype(jnp.bfloat16)
                high[i, p, :, lanes] = rounded
                low[i, p, :, lanes] = (value - rounded.astype(jnp.float32)).astype(jnp.bfloat16)
    if stage == "first":
        turn = jnp.full((8, LANES), frequency[place[0]], jnp.int32).astype(jnp.float32)
        sine = jnp.sin(turn * (math.pi / (2 * NY)))[:1]
        half_row = lax.broadcasted_iota(jnp.int32, (rows // 2, LANES), 0)
        half_kz = x_rank * rows + half_row + BLOCKS * lax.shift_right_logical(half_row, 3)
        kz_index = jnp.concatenate([half_kz, half_kz + BLOCKS], axis=0)
        row_part = -(4.0 * sine * sine + eigenvalue(kz_index, rows * x_count) + SCREEN_WEIGHT)
    dot = functools.partial(jnp.dot, preferred_element_type=jnp.float32)
    count = table.shape[4]
    width = 256
    per_row = 2 * count // LANES
    copies = []
    bands = finished.shape[0] if stage == "last" else 1
    band = rows // bands
    for n in range(bands):
        here = slice(n * band, (n + 1) * band)
        if stage == "last":
            there = slice(side_rows * rows + n * band, side_rows * rows + (n + 1) * band)
        for p in range(2):
            for c in range(count // width):
                cols = slice(c * width, (c + 1) * width)
                value = None if stage == "first" else total[p, there if stage == "last" else here, cols]
                for i, left in enumerate(lefts):
                    for data, level in ((high, 0), (low, 0), (high, 1)):
                        term = dot(data[i, p, here, :], table[level, p, left, :, cols])
                        value = term if value is None else value + term
                if stage == "first":
                    below = jnp.concatenate([row_part] * (width // LANES), axis=1) + col_part[p : p + 1, cols]
                    factor_out[p, :, cols] = 1.0 / below
                if stage != "last":
                    out[p, :, cols] = value
                    continue
                value *= factor[p, there, cols]
                for t in range(width // LANES):
                    tile = c * (width // LANES) + t
                    part = value[:, t * LANES : (t + 1) * LANES]
                    finished[n, pl.ds(2 * tile + p, band, stride=per_row), :] = part
        if stage == "last":
            block = BLOCKS * per_row
            for m in range(band // BLOCKS):
                to = pl.ds((2 * (n * (band // BLOCKS) + m) + side_rows) * block, block)
                source = finished.at[n, pl.ds(m * block, block)]
                copies.append(pltpu.make_async_copy(source, out.at[to], copied.at[len(copies)]))
                copies[-1].start()
    for copy in copies:
        copy.wait()


def x_transform(stage, place, pairs, pieces, table, extra, side_rows=None, written=None):
    halved = [e for e in pieces if isinstance(pieces[e], tuple)]
    chosen = []
    for pair in pairs:
        for e in pair:
            chosen += pieces[e] if e in halved else [pieces[e]]
    rows = pieces[0].shape[0] - META
    line_count = rows * 2 * table.shape[4] // LANES
    aliases = {}
    if stage == "last":
        rows //= 2
    if written is not None:
        extra = (*extra, written)
        aliases = {1 + len(chosen) + 1 + 2: 0}
    chunk = chosen[0].shape[1]
    count = table.shape[4]
    vmem = pl.BlockSpec(memory_space=pltpu.VMEM)
    smem = pl.BlockSpec(memory_space=pltpu.SMEM)
    sums = jax.ShapeDtypeStruct((2, rows, count), jnp.float32)
    scratch = [
        pltpu.VMEM((len(pairs), 2, chunk // LANES, rows, LANES), jnp.float32),
        pltpu.VMEM((len(pairs), 2, rows, chunk), jnp.bfloat16),
        pltpu.VMEM((len(pairs), 2, rows, chunk), jnp.bfloat16),
    ]
    out_shape, out_specs = sums, vmem
    if stage == "first":
        out_shape, out_specs = [sums, sums], [vmem, vmem]
    elif stage == "last":
        out_shape = jax.ShapeDtypeStruct((line_count, LANES), jnp.float32)
        out_specs = pl.BlockSpec(memory_space=pltpu.HBM)
        bands = 2
        scratch += [pltpu.VMEM((bands, line_count // 2 // bands, LANES), jnp.float32)]
        scratch += [pltpu.SemaphoreType.DMA((rows // BLOCKS,))]
    return pl.pallas_call(
        functools.partial(x_kernel, stage, pairs, halved, side_rows),
        in_specs=[smem] + [vmem] * (len(chosen) + 1) + ([smem, vmem] if stage == "first" else [vmem] * min(len(extra), 2) + [out_specs] * len(aliases)),
        out_specs=out_specs,
        out_shape=out_shape,
        input_output_aliases=aliases,
        scratch_shapes=scratch,
        compiler_params=pltpu.CompilerParams(vmem_limit_bytes=SCOPED),
        cost_estimate=pl.CostEstimate(
            flops=12 * rows * len(pairs) * chunk * count, bytes_accessed=16 * rows * count, transcendentals=0
        ),
        name="x_transform",
    )(place, *chosen, table, *extra)


def sent(piece, axis, d):
    return lax.ppermute(piece, axis, [(i, i ^ d) for i in range(lax.axis_size(axis))])


def shards(flux_xface, flux_yspec, flux_zface, frequency_y):
    z_count = lax.axis_size("gz")
    x_count = lax.axis_size("xy")
    y_count, planes, x_width = flux_xface.shape
    length_z, length_x = planes * z_count, x_width * x_count
    fits = z_count == BLOCKS and y_count == BLOCKS and x_count == 4 and x_width == 4 * LANES
    if not fits or planes % GROUP or planes // GROUP + 3 > META or planes != 2 * LANES or length_z != RESIDUES * GROUP * x_count:
        return plain_shards(flux_xface, flux_yspec, flux_zface, frequency_y)
    z_rank, x_rank = lax.axis_index("gz"), lax.axis_index("xy")
    place = jnp.stack([z_rank, jnp.int32(z_count), x_rank, jnp.int32(x_count)]).astype(jnp.int32)
    fluxes = (flux_xface, flux_yspec, flux_zface)
    inner, outer = (1, 2), (0, 3)
    whole = (0, x_width)
    inner_spans, outer_spans = (whole, (LANES, 3 * LANES)), (whole, whole)
    tables_z = z_tables(length_z)
    early, late = (6, 7, 2, 4), (3, 5, 1, 0)
    pieces = divergence(inner, inner_spans, early, place, frequency_y, fluxes, True)
    place_later, *pieces = lax.optimization_barrier((place, *pieces))
    first = {d: sent(piece, "gz", d) for d, piece in zip(early, pieces)}
    pieces = divergence(inner, inner_spans, late, place_later, frequency_y, fluxes, True)
    place_later, *pieces = lax.optimization_barrier((place, *pieces))
    first |= {d: sent(piece, "gz", d) if d else piece for d, piece in zip(late, pieces)}
    ahead = divergence(outer, outer_spans, range(BLOCKS), place_later, frequency_y, fluxes, False, True)
    ahead, first = lax.optimization_barrier((ahead, first))
    first = z_transform(place, [first[d] for d in range(BLOCKS)], tables_z, x_count)
    first = {0: first[0], 1: sent(first[1], "xy", 1), 2: sent(first[2], "xy", 2), 3: sent(first[3], "xy", 3), 4: first[4]}
    second = [ahead[0]] + [sent(ahead[u], "gz", 2 * u) for u in (1, 2)]
    last = ahead[3]
    second.append(sent(last, "gz", 6))
    second, first[1], first[3], first[2] = lax.optimization_barrier((second, first[1], first[3], first[2]))
    first[4] = sent(first[4], "xy", 2)
    second.append(sent(jnp.concatenate([a[1:] for a in second], axis=0), "gz", 1))
    second = z_transform(place, second, tables_z, x_count, (first[1], first[3]))
    later, latest = second[2], second[4]
    second = {0: second[0]} | {e: sent(second[e], "xy", e) for e in (3, 1)}
    kz_count = length_z // x_count
    halved = length_x // 2
    kx_index = 2 * np.arange(halved)[None, :] + np.arange(2)[:, None]
    col_part = np.asarray(-4.0 * np.sin(kx_index * (math.pi / (2 * length_x))) ** 2, np.float32)
    outside, inside = (0, 3), (1, 2)
    inner_table = x_tables(length_x, x_count // 2, x_width, inner)
    outer_table = x_tables(length_x, x_count // 2, x_width, outer)
    first = {0: first[0], 1: first[1], 2: (first[2], first[4]), 3: first[3]}
    total, factor = x_transform("first", place, (outside,), first, inner_table, (frequency_y, col_part))
    later, total = lax.optimization_barrier((later, total))
    second |= {2: sent(later, "xy", 2)}
    total = x_transform("more", place, (inside,), first, inner_table, (total,))
    total = x_transform("more", place, (outside,), second, outer_table, (total,))
    latest, total = lax.optimization_barrier((latest, total))
    latest = sent(latest, "xy", 2)
    flat = x_transform("last", place, (inside,), second, outer_table, (total, factor), 0)
    second[2] = latest
    flat = x_transform("last", place, (inside,), second, outer_table, (total, factor), 1, flat)
    tiles = halved // LANES
    return flat.reshape(1, kz_count, tiles, 2, LANES).transpose(0, 1, 3, 2, 4).reshape(1, kz_count, 2, halved)


def solution(mesh):
    return jax.shard_map(
        shards,
        mesh=mesh,
        in_specs=(P(None, "gz", "xy"), P(None, "gz", "xy"), P(None, "gz", "xy"), P()),
        out_specs=P("gz", "xy", None, None),
        check_vma=False,
    )
```
